512 devices in a mesh: section: 16 (over y, core), dp: 32 (over z, x).
Axes of the slice: x: 4, y: 8, z: 8, core: 2. Of those that a mesh axis runs over, the one named last changes fastest.
Arguments:
- first_activations: bfloat16 [4096, 4096], P('dp', 'section')
- loss_sensitivity: bfloat16 [4096, 4096], P('dp', 'section'), may hold values from -0.25 to 0.25
- computing_worker: int32 [32, 8], replicated, may hold values from 0 to 31, as said below
- scaling_factor: float32 [16, 4096], P('section'), may hold values from 0.1 to 1.9
- narrowing_weights: bfloat16 [16, 64, 4096], P('section', None, 'dp'), may hold values from -0.09375 to 0.09375
- widening_weights: bfloat16 [16, 64, 4096], P('section', None, 'dp'), may hold values from -0.75 to 0.75
Outputs:
- saved_rstd: float32 [16, 32, 160], P('section', 'dp')
- saved_inputs: bfloat16 [16, 32, 160, 4096], P('section', 'dp')
- grad_down: float32 [16, 64, 4096], P('section', None, 'dp')
- grad_up: float32 [16, 64, 4096], P('section', None, 'dp')
The draws below stay inside these ranges and needn't reach their ends.
Inputs may be any that keep to these rules, and one draw needn't show every extreme that they name: `computing_worker`: A replica either computes all its 8 micro-batches itself, or is one of 4 failed replicas whose micro-batches all go elsewhere: its micro-batches 2j and 2j + 1 go together to one replica that is not failed, and no replica takes more than one such pair. A failed replica computes none, so each replica computes 0, 8 or 10 micro-batches, and 10 occurs in every draw.
All inputs are finite; a program needn't handle non-finite values.
Results may differ from the reference program's by a relative error of at most 0.035.
Values may be sent and summed in bfloat16 or wider, within the bound.
No kernel may reach another device: no remote copies, remote signals or barrier semaphores. Data moves between devices by JAX's collectives and lax.ppermute only.
A program may use at most 64 MiB of HBM per device.

```python
import math
import jax
import jax.numpy as jnp
from jax import lax

D = 4096
RANK = 64
MB = 8
TOK = 16
SECTIONS = 16
WORKER_COPIES = 32
FAILED = 4
MICROBATCH_ROOM = 10
ROWS = 4096
N_SECTION = 16


def draw_first_activations(key, part):
    key = jax.random.fold_in(key, 11)
    first, second, third = jax.random.split(key, 3)
    row_scale = jnp.exp(jax.random.uniform(first, (ROWS, 1), jnp.float32, 0.0, math.log(10.0)))
    column_scale = jnp.exp(jax.random.uniform(second, (1, D), jnp.float32, 0.0, math.log(10.0)))
    value_rows = jax.random.normal(third, (ROWS, D), jnp.float32) * row_scale * column_scale * 0.1
    return value_rows.astype(jnp.bfloat16)


def draw_computing_worker(key, part):
    key = jax.random.fold_in(key, 5)
    first, second, third = jax.random.split(key, 3)
    count = WORKER_COPIES
    half = count // 2
    leader = jax.random.randint(first, (), 0, count).astype(jnp.int32)
    next_taker = (leader + 1) % count
    far_taker = (leader + half) % count
    everyone = jnp.arange(count, dtype=jnp.int32)
    excluded = (everyone == leader) | (everyone == next_taker) | (everyone == far_taker)
    shuffled = jax.random.permutation(second, count).astype(jnp.int32)
    order_key = jnp.where(excluded, count + shuffled, shuffled)
    ordered = jnp.argsort(order_key, stable=True).astype(jnp.int32)
    other_failed = ordered[:FAILED - 1]
    pool = ordered[FAILED - 1:count - 3]
    pair_count = FAILED * (MB // 2)
    pool_pick = pool[jax.random.permutation(third, count - FAILED - 2)[:pair_count - 2]]
    takers = jnp.concatenate([jnp.stack([next_taker, far_taker]), pool_pick]).astype(jnp.int32)
    failed = jnp.concatenate([leader[None], other_failed]).astype(jnp.int32)
    identity_rows = jnp.broadcast_to(everyone[:, None], (count, MB))
    taken_rows = jnp.repeat(takers.reshape(FAILED, MB // 2), 2, axis=1, total_repeat_length=MB)
    return identity_rows.at[failed].set(taken_rows.astype(jnp.int32))


def block_scale(stream_key, shape, pieces, smallest, largest):
    loudness = 1.0
    for position, shards_of in pieces:
        heights = jax.random.uniform(jax.random.fold_in(jax.random.fold_in(stream_key, 6), position), (shards_of,), jnp.float32, smallest / len(pieces), largest / len(pieces))
        loudness = loudness * jnp.repeat(jnp.exp(heights), shape[position] // shards_of).reshape((-1,) + (1,) * (len(shape) - 1 - position))
    return loudness


def noise(key, extent, scale, bound, shards=(), kind=jnp.bfloat16):
    array = scale * jax.random.normal(key, extent, jnp.float32)
    if shards:
        array = array * block_scale(key, extent, shards, -0.22, 0.18)
    return jnp.clip(array, -bound, bound).astype(kind)


def setup_inputs(seed: int = 0) -> dict:
    key_list = jax.random.split(jax.random.key(seed), 7)
    first_activations = draw_first_activations(jax.random.fold_in(key_list[6], 71), 0)
    loss_sensitivity = noise(key_list[1], (ROWS, D), (ROWS ** -0.5), 0.25, ((0, 32), (1, 16)))
    computing_worker = draw_computing_worker(jax.random.fold_in(key_list[6], 71), 0)
    scaling_factor = jnp.clip(1.0 + 0.18 * jax.random.normal(key_list[3], (SECTIONS, D), jnp.float32), 0.1, 1.9)
    narrowing_weights = noise(key_list[4], (SECTIONS, RANK, D), D ** -0.5, 0.09375, ((0, 16), (2, 32)))
    widening_weights = noise(key_list[5], (SECTIONS, RANK, D), RANK ** -0.5, 0.75, ((0, 16), (2, 32)))
    return {"first_activations": first_activations, "loss_sensitivity": loss_sensitivity, "computing_worker": computing_worker, "scaling_factor": scaling_factor, "narrowing_weights": narrowing_weights, "widening_weights": widening_weights}


EPS = 1e-05

def forward_section(inputs, gain_row, down_weight, up_weight):
    value_rows = inputs.astype(jnp.float32)
    inverse_norm = lax.rsqrt(lax.optimization_barrier(jnp.mean(value_rows * value_rows, axis=-1, keepdims=True)) + EPS)
    normalized_input = (value_rows * inverse_norm * gain_row).astype(jnp.bfloat16)
    preact = lax.dot_general(normalized_input, down_weight, (((1,), (1,)), ((), ())), preferred_element_type=jnp.float32)
    hidden_state = jax.nn.silu(preact).astype(jnp.bfloat16)
    output = (value_rows + jnp.dot(hidden_state, up_weight, preferred_element_type=jnp.float32)).astype(jnp.bfloat16)
    return (output, inverse_norm, normalized_input, preact, hidden_state)

def backward_section(inputs, gain_row, down_weight, up_weight, upstream_gradient):
    output, inverse_norm, normalized_input, preact, hidden_state = forward_section(inputs, gain_row, down_weight, up_weight)
    dhidden = lax.dot_general(upstream_gradient, up_weight, (((1,), (1,)), ((), ())), preferred_element_type=jnp.float32)
    sigmoid = jax.nn.sigmoid(preact)
    preactivation_gradient = (dhidden * sigmoid * (1.0 + preact * (1.0 - sigmoid))).astype(jnp.bfloat16)
    dnormed = jnp.dot(preactivation_gradient, down_weight, preferred_element_type=jnp.float32)
    scaled = dnormed * gain_row
    unit_rows = inputs.astype(jnp.float32) * inverse_norm
    dinputs = (upstream_gradient.astype(jnp.float32) + inverse_norm * (scaled - unit_rows * lax.optimization_barrier(jnp.mean(scaled * unit_rows, axis=-1, keepdims=True)))).astype(jnp.bfloat16)
    return (dinputs, normalized_input, hidden_state, preactivation_gradient)

def place_table(computing_worker, worker_sequence, place_tally):
    merged_lines = computing_worker.reshape(-1)
    entries = merged_lines.shape[0]
    owners = jnp.arange(worker_sequence, dtype=jnp.int32)
    member = (merged_lines[:, None] == owners[None, :]).astype(jnp.int32)
    places = lax.optimization_barrier(jnp.sum((jnp.cumsum(member, axis=0) - 1) * member, axis=1))
    matches = (merged_lines[:, None, None] == owners[None, :, None]) & (places[:, None, None] == jnp.arange(place_tally, dtype=jnp.int32)[None, None, :])
    filled = jnp.any(matches, axis=0)
    micro_ids = jnp.arange(entries, dtype=jnp.int32)
    sender_workers = lax.optimization_barrier(jnp.sum(matches.astype(jnp.int32) * micro_ids[:, None, None], axis=0)) + entries * (1 - filled.astype(jnp.int32))
    return sender_workers

def reference(first_activations, loss_sensitivity, computing_worker, scaling_factor, narrowing_weights, widening_weights):
    sender_workers = place_table(computing_worker, WORKER_COPIES, MICROBATCH_ROOM)
    blocks = WORKER_COPIES * MB

    def bearer_rows(value_rows):
        width = value_rows.shape[-1]
        padded = jnp.concatenate([value_rows.reshape(blocks, TOK, width), jnp.zeros((1, TOK, width), value_rows.dtype)], axis=0)
        return jnp.take(padded, sender_workers.reshape(-1), axis=0).reshape(WORKER_COPIES, MICROBATCH_ROOM * TOK, width)
    states = first_activations
    stored = []
    saved_state = []
    saved_rows = []
    for section_index in range(N_SECTION):
        stored.append(states)
        saved_rows.append(bearer_rows(states))
        states, inverse_norm, normalized_input, preact, hidden_state = forward_section(states, scaling_factor[section_index], narrowing_weights[section_index], widening_weights[section_index])
        saved_state.append(bearer_rows(inverse_norm)[:, :, 0])
    saved_rstd = jnp.stack(saved_state)
    saved_inputs = jnp.stack(saved_rows)
    upstream_gradient = loss_sensitivity
    grads_down = []
    grads_up = []
    for section_index in reversed(range(N_SECTION)):
        dinputs, normalized_input, hidden_state, preactivation_gradient = backward_section(stored[section_index], scaling_factor[section_index], narrowing_weights[section_index], widening_weights[section_index], upstream_gradient)
        up_portion = jnp.einsum('lxz,lxy->lzy', bearer_rows(hidden_state).astype(jnp.float32), bearer_rows(upstream_gradient).astype(jnp.float32), precision=lax.Precision.HIGHEST)
        down_portion = jnp.einsum('lxz,lxy->lzy', bearer_rows(preactivation_gradient).astype(jnp.float32), bearer_rows(normalized_input).astype(jnp.float32), precision=lax.Precision.HIGHEST)
        grads_up.append(lax.optimization_barrier(jnp.sum(lax.optimization_barrier(up_portion.astype(jnp.bfloat16)).astype(jnp.float32), axis=0)))
        grads_down.append(lax.optimization_barrier(jnp.sum(lax.optimization_barrier(down_portion.astype(jnp.bfloat16)).astype(jnp.float32), axis=0)))
        upstream_gradient = dinputs
    grad_down = jnp.stack(grads_down[::-1])
    grad_up = jnp.stack(grads_up[::-1])
    return (saved_rstd, saved_inputs, grad_down, grad_up)
```

```python
import jax
import jax.numpy as jnp
from jax import lax
from jax.experimental import pallas as pl
from jax.experimental.pallas import tpu as pltpu
from jax.sharding import PartitionSpec as P


EPS = 1e-05
SECT = 16
DP = 32
RANK = 64
D = 4096
F = 256
ROWS = 128
PAIR = 32
PIECE = 4224
BACK = 2432
GW = 1152
F32 = jnp.float32
BF = jnp.bfloat16
NT = (((1,), (1,)), ((), ()))
NN = (((1,), (0,)), ((), ()))
Y_GROUPS = [[2 * y + c for y in range(8)] for c in range(2)]
VMEM_LIMIT = 48 * 1024 * 1024


def dot(a, b, dims):
    return lax.dot_general(a, b, dims, preferred_element_type=F32)


def hi_lo(v):
    hi = v.astype(BF).astype(F32)
    return hi, v - hi


def vmem(n):
    return [pl.BlockSpec(memory_space=pltpu.VMEM)] * n


SMEM = pl.BlockSpec(memory_space=pltpu.SMEM)


def project_kernel(ints, x_ref, pair_ref, g_ref, w_ref, out_ref, wc_ref, uc_ref, ex_ref, gr_ref, mi_ref):
    for s in range(SECT):
        for h in range(2):
            block = w_ref[2 * s + h]
            lanes = slice(128 * h, 128 * h + 128)
            wc_ref[128 * s : 128 * s + 128, lanes] = block
            uc_ref[64 * s : 64 * s + 64, lanes] = block[64:128]
    x = x_ref[...]
    pair = pair_ref[...]
    out_ref[:, 0:2048] = dot(x, wc_ref[...], NT).astype(BF)
    out_ref[:, 2048:3072] = dot(g_ref[...], uc_ref[...], NT).astype(BF)
    extra = dot(pair, wc_ref[...], NT)
    for i in range(2):
        for k in range(4):
            for b in range(4):
                at = 512 * k + 128 * b
                ex_ref[pl.ds(128 * b + 4 * i + k, 16, stride=8), :] = extra[16 * i : 16 * i + 16, at : at + 128]
    for b in range(4):
        out_ref[:, 3072 + 128 * b : 3200 + 128 * b] = ex_ref[128 * b : 128 * b + 128, :].astype(BF)

    p = ints[0]
    quarter = ints[1]
    m = p // 2 + 1
    small_rows = wc_ref[pl.ds(pl.multiple_of(128 * p + 32 * quarter, 32), 32), :]
    big_rows = wc_ref[pl.ds(pl.multiple_of(128 * (15 - p) + 32 * quarter, 32), 32), :]
    small = dot(small_rows, uc_ref[0:512, :], NT)
    big = dot(big_rows, uc_ref[...], NT)
    st = [small[:, 128 * t : 128 * t + 128] for t in range(4)]
    tiles = [big[:, 128 * t : 128 * t + 128] for t in range(8)]
    tiles.append(st[3])
    for t in range(5, 9):
        for mm in range(1, 5):
            j = t - (9 - mm)
            if 0 <= j < 4:
                tiles[t] = jnp.where(m == mm, st[j], tiles[t])
    gr_ref[...] = jnp.zeros_like(gr_ref)
    for c in range(2):
        for y in range(8):
            rows = slice(8 * (2 * y + c), 8 * (2 * y + c) + 8)
            for b in range(2 if y == 7 else 1):
                tile = tiles[y + b]
                gr_ref[rows, 128 * b : 128 * b + 128] = tile[16 * c : 16 * c + 8]
                gr_ref[rows, 256 + 128 * b : 384 + 128 * b] = tile[16 * c + 8 : 16 * c + 16]
    out_ref[:, 3584:4096] = gr_ref[...].astype(BF)

    xf = x.astype(F32)
    pf = pair.astype(F32)
    own_hi, own_lo = hi_lo(jnp.sum(xf * xf, axis=1, keepdims=True))
    pair_hi, pair_lo = hi_lo(jnp.sum(pf * pf, axis=1, keepdims=True))
    mi_ref[...] = jnp.zeros_like(mi_ref)
    lane = lax.broadcasted_iota(jnp.int32, (PAIR, 128), 1)
    pair_part = jnp.where(lane == 2, pair_hi, 0.0) + jnp.where(lane == 3, pair_lo, 0.0)
    for i in range(2):
        mi_ref[pl.ds(i, 16, stride=8), :] = pair_part[16 * i : 16 * i + 16]
    lane = lax.broadcasted_iota(jnp.int32, (ROWS, 128), 1)
    own_part = jnp.where(lane == 0, own_hi, 0.0) + jnp.where(lane == 1, own_lo, 0.0)
    out_ref[:, 4096:4224] = (mi_ref[...] + own_part).astype(BF)


def slab_place(s):
    if s >= 8:
        return 15 - s, 0
    return s, 128 * (9 - (s // 2 + 1))


def recur_kernel(ints, sum_ref, mine_ref, other_ref, out_ref, slab_ref, pq_ref, h_ref, acc_ref, t_ref, pre_ref, ds_ref, ho_ref):
    core = ints[0]
    mine_row = pl.multiple_of(16 * core, 16)
    other_row = pl.multiple_of(16 * (1 - core), 16)
    for q in range(DP):
        base = 128 * (q // 4) + 32 * (q % 4)
        slab_ref[pl.ds(base + mine_row, 16), :] = mine_ref[q]
        slab_ref[pl.ds(base + other_row, 16), :] = other_ref[q]
    pq_ref[...] = jnp.zeros_like(pq_ref)
    pq_ref[0:8, :] = sum_ref[:, 0:3072]
    for i in range(2):
        for k in range(4):
            pq_ref[8 + i : 9 + i, 512 * k : 512 * k + 512] = sum_ref[4 * i + k : 4 * i + k + 1, 3072:3584]
    h_ref[...] = jnp.zeros_like(h_ref)
    acc_ref[...] = jnp.zeros_like(acc_ref)
    misc = sum_ref[:, 4096:4224]
    n = jnp.concatenate([misc[:, 0:1] + misc[:, 1:2], misc[:, 2:3] + misc[:, 3:4]], axis=0)
    row = lax.broadcasted_iota(jnp.int32, (16, 1), 0)
    n = jnp.where(row < 10, n, 0.0)

    inverse = []
    zeros = jnp.zeros((16, RANK), BF)
    for s in range(SECT):
        place, off = slab_place(s)
        r0 = 128 * place
        depth = 128 * ((s + 1) // 2)
        tp = pq_ref[:, 128 * s : 128 * s + 64]
        tq = pq_ref[:, 128 * s + 64 : 128 * s + 128]
        if s:
            before = h_ref[:, 0:depth]
            tp = tp + dot(before, slab_ref[r0 : r0 + 64, off : off + depth], NT)
            tq = tq + dot(before, slab_ref[r0 + 64 : r0 + 128, off : off + depth], NT)
        inv = lax.rsqrt(jnp.maximum(n, 0.0) * (1.0 / D) + EPS)
        inverse.append(inv)
        pre = inv * tp
        sig = 1.0 / (1.0 + jnp.exp(-pre))
        hf = pre * sig
        h = hf.astype(BF)
        pre_ref[:, 64 * s : 64 * s + 64] = pre
        ds_ref[:, 64 * s : 64 * s + 64] = sig * (1.0 + pre * (1.0 - sig))
        tile = slice(128 * (s // 2), 128 * (s // 2) + 128)
        own = jnp.concatenate([zeros, h] if s % 2 else [h, zeros], axis=1)
        h_ref[:, tile] = h_ref[:, tile] + own if s % 2 else own
        hd = dot(own, slab_ref[r0 + 64 : r0 + 128, off + tile.start : off + tile.stop], NT)
        n = n + jnp.sum(h.astype(F32) * (2.0 * tq + hd), axis=1, keepdims=True)
        t_ref[:, 64 * s : 64 * s + 64] = tq + hd

    lane16 = lax.broadcasted_iota(jnp.int32, (16, 128), 1)
    beta_sum = jnp.zeros((16, 1), F32)
    misc_out = jnp.zeros((16, 128), F32)
    for s in range(SECT - 1, -1, -1):
        place, off = slab_place(s)
        r0 = 128 * place
        cols = slice(64 * s, 64 * s + 64)
        inv = inverse[s]
        hf = h_ref[:, cols].astype(F32)
        dh = pq_ref[:, 2048 + 64 * s : 2048 + 64 * s + 64] + acc_ref[:, cols] - beta_sum * t_ref[:, cols]
        dp = (dh * ds_ref[:, cols]).astype(BF).astype(F32)
        beta = inv * inv * (jnp.sum(dp * pre_ref[:, cols], axis=1, keepdims=True) * (1.0 / D))
        z = (inv * dp).astype(BF)
        hb = (beta_sum * hf).astype(BF)
        depth = 128 * ((s + 1) // 2)
        for start in range(depth - 128, -1, -128):
            part = slice(start, start + 128)
            acc_ref[:, part] = (
                acc_ref[:, part]
                + dot(z, slab_ref[r0 : r0 + 64, off + start : off + start + 128], NN)
                - dot(hb, slab_ref[r0 + 64 : r0 + 128, off + start : off + start + 128], NN)
            )
        beta_sum = beta_sum + beta
        ho_ref[0:8, 1024 + 64 * s : 1024 + 64 * s + 64] = z[0:8].astype(F32)
        inv_hi, inv_lo = hi_lo(inv)
        misc_out = jnp.where(lane16 == s, beta, misc_out)
        misc_out = jnp.where(lane16 == 16 + s, inv_hi, misc_out)
        misc_out = jnp.where(lane16 == 32 + s, inv_lo, misc_out)
    h_all = h_ref[...].astype(F32)
    ho_ref[0:8, 0:1024] = h_all[0:8]
    for i in range(2):
        for k in range(4):
            ho_ref[4 * i + k : 4 * i + k + 1, 2048:2304] = h_all[8 + i : 9 + i, 256 * k : 256 * k + 256]
    extra_misc = pltpu.roll(misc_out[8:16], 32, 1)
    lane8 = lax.broadcasted_iota(jnp.int32, (8, 128), 1)
    row8 = lax.broadcasted_iota(jnp.int32, (8, 128), 0)
    keep = (lane8 >= 48) & (lane8 < 80) & (row8 < 2)
    ho_ref[0:8, 2304:2432] = jnp.where(keep, extra_misc, jnp.where(lane8 < 48, misc_out[0:8], 0.0))
    out_ref[...] = ho_ref[...].astype(BF)


def rebuild_kernel(ints, x_ref, pair_ref, back_ref, eh_ref, wc_ref, out_ref):
    own_at = pl.multiple_of(ints[0], 32)
    pair_at = pl.multiple_of(ints[1], 32)
    alive = ints[2] > 0
    x = x_ref[...].astype(F32)
    e = pair_ref[...].astype(F32)
    for s in range(SECT):
        out_ref[s, pl.ds(own_at, ROWS), :] = jnp.where(alive, x, 0.0).astype(BF)
        out_ref[s, pl.ds(pair_at, PAIR), :] = e.astype(BF)
        if s < SECT - 1:
            up = wc_ref[128 * s + 64 : 128 * s + 128, :]
            x = x + dot(back_ref[:, 64 * s : 64 * s + 64], up, NN)
            e = e + dot(eh_ref[:, 64 * s : 64 * s + 64], up, NN)


def grads_kernel(x_ref, g_ref, back_ref, wc_ref, out_ref, xs_ref, ht_ref, zt_ref):
    ht_ref[...] = back_ref[:, 0:1024].T
    zt_ref[...] = back_ref[:, 1024:2048].T
    x = x_ref[...].astype(F32)
    for s in range(SECT):
        xs_ref[s] = x.astype(BF)
        if s < SECT - 1:
            x = x + dot(back_ref[:, 64 * s : 64 * s + 64], wc_ref[128 * s + 64 : 128 * s + 128, :], NN)
    g = g_ref[...].astype(F32)
    betas = back_ref[:, 2304:2432].astype(F32)
    for s in range(SECT - 1, -1, -1):
        xs = xs_ref[s]
        up = dot(ht_ref[64 * s : 64 * s + 64, :], g.astype(BF), NN).astype(BF)
        down = dot(zt_ref[64 * s : 64 * s + 64, :], xs, NN).astype(BF)
        for h in range(2):
            lanes = slice(128 * h, 128 * h + 128)
            out_ref[2 * s + h, 0:64, :] = up[:, lanes]
            out_ref[2 * s + h, 64:128, :] = down[:, lanes]
        if s:
            z = back_ref[:, 1024 + 64 * s : 1024 + 64 * s + 64]
            g = g + dot(z, wc_ref[128 * s : 128 * s + 64, :], NN) - betas[:, s : s + 1] * xs.astype(F32)


def call(kernel, n_in, outs, scratch, flops, nbytes, with_ints=True):
    return pl.pallas_call(
        kernel,
        out_shape=outs,
        in_specs=([SMEM] if with_ints else []) + vmem(n_in),
        out_specs=jax.tree.map(lambda _: pl.BlockSpec(memory_space=pltpu.VMEM), outs),
        scratch_shapes=scratch,
        compiler_params=pltpu.CompilerParams(vmem_limit_bytes=VMEM_LIMIT),
        cost_estimate=pl.CostEstimate(flops=flops, bytes_accessed=nbytes, transcendentals=0),
    )


def shape(*dims, kind=BF):
    return jax.ShapeDtypeStruct(dims, kind)


def exchange(value, axis, groups=None):
    return lax.all_to_all(value, axis, 0, 0, tiled=True, axis_index_groups=groups)


def body(x, g, worker, gain, narrow, widen):
    sec = lax.axis_index("section")
    me = lax.axis_index("dp")

    gain_here = lax.dynamic_slice(gain, (0, 128 * me), (1, 128))
    block = jnp.concatenate([(narrow[0].astype(F32) * gain_here).astype(BF), widen[0]], axis=0)
    there = [(s * DP + d, (d // 2) * DP + 2 * s + d % 2) for s in range(SECT) for d in range(DP)]
    back_again = [(b, a) for a, b in there]
    block = lax.ppermute(block, ("section", "dp"), there)

    owners = jnp.arange(DP, dtype=jnp.int32)
    takers = worker[:, ::2]
    mine = lax.dynamic_index_in_dim(takers, me, 0, keepdims=False)
    alive = mine[0] == me
    goes = (mine[None, :] == owners[:, None]) & jnp.logical_not(alive)
    quads = x.reshape(4, PAIR, F)
    outgoing = jnp.zeros((DP, PAIR, F), BF)
    for j in range(4):
        outgoing = jnp.where(goes[:, j][:, None, None], quads[j][None], outgoing)
    arrived = exchange(outgoing, "dp")
    comes = jnp.any((takers == me) & (owners != me)[:, None], axis=1)
    source = jnp.sum(jnp.where(comes, owners, 0))
    taking = jnp.any(comes)
    pair = lax.dynamic_index_in_dim(arrived, source, 0, keepdims=False)
    pair = jnp.where(taking, pair, jnp.zeros_like(pair))
    pair_first = taking & (source < me)

    weights = exchange(jnp.broadcast_to(block[None], (DP, 128, 128)), "dp")
    pieces, wc = call(
        project_kernel,
        4,
        (shape(ROWS, PIECE), shape(2048, F)),
        [
            pltpu.VMEM((1024, F), BF),
            pltpu.VMEM((4 * ROWS, 128), F32),
            pltpu.VMEM((ROWS, 512), F32),
            pltpu.VMEM((ROWS, 128), F32),
        ],
        3 * 10**8,
        3 * 10**6,
    )(jnp.stack([me // 4, me % 4]).astype(jnp.int32), x, pair, g, weights)
    pieces = exchange(pieces.reshape(SECT, 8, PIECE), "section")
    total = jnp.sum(pieces.astype(F32), axis=0)

    share = jnp.concatenate([total[:, 3584:3840], total[:, 3840:4096]], axis=0).astype(BF)
    share = exchange(jnp.broadcast_to(share[None], (8, 16, 256)), "section", Y_GROUPS)
    share = jnp.concatenate([share[y, :, 0:128] for y in range(8)] + [share[7, :, 128:256]], axis=1)
    half = exchange(jnp.broadcast_to(share[None], (DP, 16, GW)), "dp")
    other = lax.ppermute(half, "section", [(i, i ^ 1) for i in range(SECT)])

    back = call(
        recur_kernel,
        3,
        shape(8, BACK),
        [
            pltpu.VMEM((1024, GW), BF),
            pltpu.VMEM((16, 3072), F32),
            pltpu.VMEM((16, 1024), BF),
            pltpu.VMEM((16, 1024), F32),
            pltpu.VMEM((16, 1024), F32),
            pltpu.VMEM((16, 1024), F32),
            pltpu.VMEM((16, 1024), F32),
            pltpu.VMEM((8, BACK), F32),
        ],
        2 * 10**8,
        3 * 10**6,
    )((sec % 2).reshape(1).astype(jnp.int32), total, half, other)
    back = exchange(jnp.broadcast_to(back[None], (SECT, 8, BACK)), "section")

    grads = call(
        grads_kernel,
        4,
        shape(DP, 128, 128),
        [pltpu.VMEM((SECT, ROWS, F), BF), pltpu.VMEM((1024, ROWS), BF), pltpu.VMEM((1024, ROWS), BF)],
        3 * 10**8,
        3 * 10**6,
        False,
    )(x, g, back.reshape(ROWS, BACK), wc)
    grads = exchange(grads, "dp")
    grads = jnp.sum(grads.astype(F32), axis=0)
    grads = lax.ppermute(grads, ("section", "dp"), back_again)

    extra_h = back[:, :, 2048:2304].reshape(SECT, 2, 4, 256).transpose(1, 0, 2, 3).reshape(PAIR, 1024)
    own_at = jnp.where(pair_first, PAIR, 0)
    pair_at = jnp.where(pair_first, 0, ROWS)
    rows_out = call(
        rebuild_kernel,
        5,
        shape(SECT, ROWS + PAIR, F),
        [],
        2 * 10**8,
        3 * 10**6,
    )(jnp.stack([own_at, pair_at, alive.astype(jnp.int32)]).astype(jnp.int32), x, pair, back.reshape(ROWS, BACK), extra_h, wc)
    saved = exchange(rows_out, "section")
    saved = saved.transpose(1, 0, 2).reshape(1, 1, ROWS + PAIR, D)

    misc = back[:, :, 2304:2432].astype(F32)
    own_inv = misc[:, :, 16:32] + misc[:, :, 32:48]
    pair_inv = misc[:, 0:2, 48:64] + misc[:, 0:2, 64:80]
    own_inv = lax.dynamic_index_in_dim(own_inv, sec, 2, keepdims=False).reshape(ROWS)
    pair_inv = lax.dynamic_index_in_dim(pair_inv, sec, 2, keepdims=False).T.reshape(PAIR)
    own_inv = jnp.where(alive, own_inv, 0.0)
    pair_inv = jnp.where(taking, pair_inv, 0.0)
    rstd = jnp.where(
        pair_first, jnp.concatenate([pair_inv, own_inv]), jnp.concatenate([own_inv, pair_inv])
    ).reshape(1, 1, ROWS + PAIR)
    return rstd, saved, (grads[64:128] * gain_here)[None], grads[0:64][None]


def solution(mesh):
    in_specs = (
        P("dp", "section"),
        P("dp", "section"),
        P(),
        P("section", None),
        P("section", None, "dp"),
        P("section", None, "dp"),
    )
    out_specs = (
        P("section", "dp", None),
        P("section", "dp", None, None),
        P("section", None, "dp"),
        P("section", None, "dp"),
    )
    return jax.shard_map(body, mesh=mesh, in_specs=in_specs, out_specs=out_specs, check_vma=False)
```

```python
import jax
import jax.numpy as jnp
from jax import lax
from jax.experimental import pallas as pl
from jax.experimental.pallas import tpu as pltpu
from jax.sharding import PartitionSpec as P


EPS = 1e-05
SECT = 16
DP = 32
RANK = 64
D = 4096
F = 256
ROWS = 128
PAIR = 32
PIECE = 3712
BACK = 2432
GW = 1152
F32 = jnp.float32
BF = jnp.bfloat16
NT = (((1,), (1,)), ((), ()))
NN = (((1,), (0,)), ((), ()))
Y_GROUPS = [[2 * y + c for y in range(8)] for c in range(2)]
VMEM_LIMIT = 48 * 1024 * 1024


def dot(a, b, dims):
    return lax.dot_general(a, b, dims, preferred_element_type=F32)


def hi_lo(v):
    hi = v.astype(BF).astype(F32)
    return hi, v - hi


def vmem(n):
    return [pl.BlockSpec(memory_space=pltpu.VMEM)] * n


SMEM = pl.BlockSpec(memory_space=pltpu.SMEM)


def project_kernel(ints, x_ref, g_ref, w_ref, keep_ref, send_ref, wc_ref, pair_ref, uc_ref, res_ref, gr_ref, ex_ref):
    p, quarter, core, source = ints[0], ints[1], ints[2], ints[3]
    taking = ints[4] > 0
    for s in range(SECT):
        for h in range(2):
            block = w_ref[2 * s + h, 0:128, :]
            lanes = slice(128 * h, 128 * h + 128)
            wc_ref[128 * s : 128 * s + 128, lanes] = block
            uc_ref[64 * s : 64 * s + 64, lanes] = block[64:128]
    for h in range(2):
        part = w_ref[source, 128 + 32 * h : 160 + 32 * h, :]
        pair_ref[:, 128 * h : 128 * h + 128] = jnp.where(taking, part, jnp.zeros_like(part))

    x = x_ref[...]
    pair = pair_ref[...]
    res_ref[:, 0:2048] = dot(x, wc_ref[...], NT)
    res_ref[:, 2048:3072] = dot(g_ref[...], uc_ref[...], NT)
    extra = dot(pair, wc_ref[...], NT)
    for i in range(2):
        for k in range(4):
            for b in range(4):
                at = 512 * k + 128 * b
                ex_ref[pl.ds(128 * b + 4 * i + k, 16, stride=8), :] = extra[16 * i : 16 * i + 16, at : at + 128]
    for b in range(4):
        res_ref[:, 3072 + 128 * b : 3200 + 128 * b] = ex_ref[128 * b : 128 * b + 128, :]

    xf = x.astype(F32)
    pf = pair.astype(F32)
    own_hi, own_lo = hi_lo(jnp.sum(xf * xf, axis=1, keepdims=True))
    pair_hi, pair_lo = hi_lo(jnp.sum(pf * pf, axis=1, keepdims=True))
    ex_ref[0:ROWS, :] = jnp.zeros((ROWS, 128), F32)
    lane = lax.broadcasted_iota(jnp.int32, (PAIR, 128), 1) - 4 * core
    pair_part = jnp.where(lane == 2, pair_hi, 0.0) + jnp.where(lane == 3, pair_lo, 0.0)
    for i in range(2):
        ex_ref[pl.ds(i, 16, stride=8), :] = pair_part[16 * i : 16 * i + 16]
    lane = lax.broadcasted_iota(jnp.int32, (ROWS, 128), 1) - 4 * core
    own_part = jnp.where(lane == 0, own_hi, 0.0) + jnp.where(lane == 1, own_lo, 0.0)
    res_ref[:, 3584:3712] = ex_ref[0:ROWS, :] + own_part

    m = p // 2 + 1
    small_rows = wc_ref[pl.ds(pl.multiple_of(128 * p + 32 * quarter, 32), 32), :]
    big_rows = wc_ref[pl.ds(pl.multiple_of(128 * (15 - p) + 32 * quarter, 32), 32), :]
    small = dot(small_rows, uc_ref[0:512, :], NT)
    big = dot(big_rows, uc_ref[...], NT)
    st = [small[:, 128 * t : 128 * t + 128] for t in range(4)]
    tiles = [big[:, 128 * t : 128 * t + 128] for t in range(8)]
    tiles.append(st[3])
    for t in range(5, 9):
        for mm in range(1, 5):
            j = t - (9 - mm)
            if 0 <= j < 4:
                tiles[t] = jnp.where(m == mm, st[j], tiles[t])
    for t in range(9):
        gr_ref[:, 128 * t : 128 * t + 128] = tiles[t]

    for ref, parity in ((keep_ref, core), (send_ref, 1 - core)):
        for y in range(0, 8, 2):
            first = res_ref[pl.ds(pl.multiple_of(16 * y + 8 * parity, 8), 8), :]
            second = res_ref[pl.ds(pl.multiple_of(16 * y + 16 + 8 * parity, 8), 8), :]
            ref[8 * y : 8 * y + 16, :] = jnp.concatenate([first, second], axis=0).astype(BF)
        ref[64:80, 0:GW] = gr_ref[pl.ds(pl.multiple_of(16 * parity, 16), 16), :].astype(BF)
        ref[64:80, GW:PIECE] = jnp.zeros((16, PIECE - GW), BF)


def slab_place(s):
    if s >= 8:
        return 15 - s, 0
    return s, 128 * (9 - (s // 2 + 1))


def recur_kernel(ints, sum_ref, mine_ref, other_ref, out_ref, slab_ref, pq_ref, h_ref, acc_ref, t_ref, pre_ref, ds_ref, ho_ref):
    core = ints[0]
    mine_row = pl.multiple_of(16 * core, 16)
    other_row = pl.multiple_of(16 * (1 - core), 16)
    for q in range(DP):
        base = 128 * (q // 4) + 32 * (q % 4)
        slab_ref[pl.ds(base + mine_row, 16), :] = mine_ref[q]
        slab_ref[pl.ds(base + other_row, 16), :] = other_ref[q]
    pq_ref[...] = jnp.zeros_like(pq_ref)
    pq_ref[0:8, :] = sum_ref[:, 0:3072]
    more = sum_ref[:, 3072:3584]
    for i in range(2):
        for k in range(4):
            pq_ref[8 + i : 9 + i, 512 * k : 512 * k + 512] = more[4 * i + k : 4 * i + k + 1]
    h_ref[...] = jnp.zeros_like(h_ref)
    acc_ref[...] = jnp.zeros_like(acc_ref)
    misc = sum_ref[:, 3584:3712]
    misc = misc + pltpu.roll(misc, 124, 1)
    n = jnp.concatenate([misc[:, 0:1] + misc[:, 1:2], misc[:, 2:3] + misc[:, 3:4]], axis=0)
    row = lax.broadcasted_iota(jnp.int32, (16, 1), 0)
    n = jnp.where(row < 10, n, 0.0)

    inverse = []
    zeros = jnp.zeros((16, RANK), BF)
    for s in range(SECT):
        place, off = slab_place(s)
        r0 = 128 * place
        depth = 128 * ((s + 1) // 2)
        tp = pq_ref[:, 128 * s : 128 * s + 64]
        tq = pq_ref[:, 128 * s + 64 : 128 * s + 128]
        if s:
            before = h_ref[:, 0:depth]
            tp = tp + dot(before, slab_ref[r0 : r0 + 64, off : off + depth], NT)
            tq = tq + dot(before, slab_ref[r0 + 64 : r0 + 128, off : off + depth], NT)
        inv = lax.rsqrt(jnp.maximum(n, 0.0) * (1.0 / D) + EPS)
        inverse.append(inv)
        pre = inv * tp
        sig = 1.0 / (1.0 + jnp.exp(-pre))
        hf = pre * sig
        h = hf.astype(BF)
        pre_ref[:, 64 * s : 64 * s + 64] = pre
        ds_ref[:, 64 * s : 64 * s + 64] = sig * (1.0 + pre * (1.0 - sig))
        tile = slice(128 * (s // 2), 128 * (s // 2) + 128)
        own = jnp.concatenate([zeros, h] if s % 2 else [h, zeros], axis=1)
        h_ref[:, tile] = h_ref[:, tile] + own if s % 2 else own
        hd = dot(own, slab_ref[r0 + 64 : r0 + 128, off + tile.start : off + tile.stop], NT)
        n = n + jnp.sum(h.astype(F32) * (2.0 * tq + hd), axis=1, keepdims=True)
        t_ref[:, 64 * s : 64 * s + 64] = tq + hd

    lane16 = lax.broadcasted_iota(jnp.int32, (16, 128), 1)
    beta_sum = jnp.zeros((16, 1), F32)
    misc_out = jnp.zeros((16, 128), F32)
    for s in range(SECT - 1, -1, -1):
        place, off = slab_place(s)
        r0 = 128 * place
        cols = slice(64 * s, 64 * s + 64)
        inv = inverse[s]
        hf = h_ref[:, cols].astype(F32)
        dh = pq_ref[:, 2048 + 64 * s : 2048 + 64 * s + 64] + acc_ref[:, cols] - beta_sum * t_ref[:, cols]
        dp = (dh * ds_ref[:, cols]).astype(BF).astype(F32)
        beta = inv * inv * (jnp.sum(dp * pre_ref[:, cols], axis=1, keepdims=True) * (1.0 / D))
        z = (inv * dp).astype(BF)
        hb = (beta_sum * hf).astype(BF)
        depth = 128 * ((s + 1) // 2)
        for start in range(depth - 128, -1, -128):
            part = slice(start, start + 128)
            acc_ref[:, part] = (
                acc_ref[:, part]
                + dot(z, slab_ref[r0 : r0 + 64, off + start : off + start + 128], NN)
                - dot(hb, slab_ref[r0 + 64 : r0 + 128, off + start : off + start + 128], NN)
            )
        beta_sum = beta_sum + beta
        ho_ref[0:8, 1024 + 64 * s : 1024 + 64 * s + 64] = z[0:8].astype(F32)
        inv_hi, inv_lo = hi_lo(inv)
        misc_out = jnp.where(lane16 == s, beta, misc_out)
        misc_out = jnp.where(lane16 == 16 + s, inv_hi, misc_out)
        misc_out = jnp.where(lane16 == 32 + s, inv_lo, misc_out)
    h_all = h_ref[...].astype(F32)
    ho_ref[0:8, 0:1024] = h_all[0:8]
    for i in range(2):
        for k in range(4):
            ho_ref[4 * i + k : 4 * i + k + 1, 2048:2304] = h_all[8 + i : 9 + i, 256 * k : 256 * k + 256]
    extra_misc = pltpu.roll(misc_out[8:16], 32, 1)
    lane8 = lax.broadcasted_iota(jnp.int32, (8, 128), 1)
    row8 = lax.broadcasted_iota(jnp.int32, (8, 128), 0)
    keep = (lane8 >= 48) & (lane8 < 80) & (row8 < 2)
    ho_ref[0:8, 2304:2432] = jnp.where(keep, extra_misc, jnp.where(lane8 < 48, misc_out[0:8], 0.0))
    out_ref[...] = ho_ref[...].astype(BF)


def rebuild_kernel(ints, x_ref, pair_ref, back_ref, eh_ref, wc_ref, out_ref):
    own_at = pl.multiple_of(ints[0], 32)
    pair_at = pl.multiple_of(ints[1], 32)
    alive = ints[2] > 0
    x = x_ref[...].astype(F32)
    e = pair_ref[...].astype(F32)
    for s in range(SECT):
        out_ref[s, pl.ds(own_at, ROWS), :] = jnp.where(alive, x, 0.0).astype(BF)
        out_ref[s, pl.ds(pair_at, PAIR), :] = e.astype(BF)
        if s < SECT - 1:
            up = wc_ref[128 * s + 64 : 128 * s + 128, :]
            x = x + dot(back_ref[:, 64 * s : 64 * s + 64], up, NN)
            e = e + dot(eh_ref[:, 64 * s : 64 * s + 64], up, NN)


def grads_kernel(ints, x_ref, g_ref, back_ref, wc_ref, keep_ref, send_ref, xs_ref, ht_ref, zt_ref):
    upper = ints[0] > 0
    ht_ref[...] = back_ref[:, 0:1024].T
    zt_ref[...] = back_ref[:, 1024:2048].T
    x = x_ref[...].astype(F32)
    for s in range(SECT):
        xs_ref[s] = x.astype(BF)
        if s < SECT - 1:
            x = x + dot(back_ref[:, 64 * s : 64 * s + 64], wc_ref[128 * s + 64 : 128 * s + 128, :], NN)
    g = g_ref[...].astype(F32)
    betas = back_ref[:, 2304:2432].astype(F32)
    for s in range(SECT - 1, -1, -1):
        xs = xs_ref[s]
        up = dot(ht_ref[64 * s : 64 * s + 64, :], g.astype(BF), NN).astype(BF)
        down = dot(zt_ref[64 * s : 64 * s + 64, :], xs, NN).astype(BF)
        for rows, value in ((slice(0, 64), up), (slice(64, 128), down)):
            keep_ref[s, rows, :] = jnp.where(upper, value[:, 128:256], value[:, 0:128])
            send_ref[s, rows, :] = jnp.where(upper, value[:, 0:128], value[:, 128:256])
        if s:
            z = back_ref[:, 1024 + 64 * s : 1024 + 64 * s + 64]
            g = g + dot(z, wc_ref[128 * s : 128 * s + 64, :], NN) - betas[:, s : s + 1] * xs.astype(F32)


def join_kernel(in_ref, out_ref):
    for k in range(SECT):
        out_ref[0, 0, :, F * k : F * k + F] = in_ref[k]


def call(kernel, n_in, outs, scratch, flops, nbytes, with_ints=True):
    return pl.pallas_call(
        kernel,
        out_shape=outs,
        in_specs=([SMEM] if with_ints else []) + vmem(n_in),
        out_specs=jax.tree.map(lambda _: pl.BlockSpec(memory_space=pltpu.VMEM), outs),
        scratch_shapes=scratch,
        compiler_params=pltpu.CompilerParams(vmem_limit_bytes=VMEM_LIMIT),
        cost_estimate=pl.CostEstimate(flops=flops, bytes_accessed=nbytes, transcendentals=0),
    )


def shape(*dims, kind=BF):
    return jax.ShapeDtypeStruct(dims, kind)


def exchange(value, axis, groups=None):
    return lax.all_to_all(value, axis, 0, 0, tiled=True, axis_index_groups=groups)


def scatter_sum(keep, send, me):
    for b in range(4):
        value = keep.astype(F32) + lax.ppermute(send, "dp", [(i, i ^ (1 << b)) for i in range(DP)]).astype(F32)
        value = value.astype(BF).reshape((value.shape[0] // 2, 2) + value.shape[1:])
        bit = (me >> (b + 1)) & 1
        keep = lax.dynamic_index_in_dim(value, bit, 1, keepdims=False)
        send = lax.dynamic_index_in_dim(value, 1 - bit, 1, keepdims=False)
    both = ("section", "dp")
    mine = lax.ppermute(keep[0], both, [(a, owner(a // DP, a % DP)) for a in range(SECT * DP)])
    theirs = lax.ppermute(send[0], both, [(a, owner(a // DP, a % DP ^ 16)) for a in range(SECT * DP)])
    return mine.astype(F32) + theirs.astype(F32)


def owner(sec, q):
    return (q // 2) * DP + 2 * sec + q % 2


def body(x, g, worker, gain, narrow, widen):
    sec = lax.axis_index("section")
    me = lax.axis_index("dp")

    gain_here = lax.dynamic_slice(gain, (0, 128 * me), (1, 128))
    block = jnp.concatenate([(narrow[0].astype(F32) * gain_here).astype(BF), widen[0]], axis=0)
    block = lax.ppermute(block, ("section", "dp"), [(owner(a // DP, a % DP), a) for a in range(SECT * DP)])

    owners = jnp.arange(DP, dtype=jnp.int32)
    takers = worker[:, ::2]
    mine = lax.dynamic_index_in_dim(takers, me, 0, keepdims=False)
    alive = mine[0] == me
    comes = jnp.any((takers == me) & (owners != me)[:, None], axis=1)
    source = jnp.sum(jnp.where(comes, owners, 0))
    taking = jnp.any(comes)
    pair_first = taking & (source < me)
    goes = (mine[None, :] == owners[:, None]) & jnp.logical_not(alive)
    quads = jnp.concatenate([x[:, 0:128].reshape(4, PAIR, 128), x[:, 128:256].reshape(4, PAIR, 128)], axis=1)
    outgoing = jnp.zeros((DP, 2 * PAIR, 128), BF)
    for j in range(4):
        outgoing = jnp.where(goes[:, j][:, None, None], quads[j][None], outgoing)
    weights = jnp.concatenate([jnp.broadcast_to(block[None], (DP, 128, 128)), outgoing], axis=1)
    weights = exchange(weights, "dp")

    core = sec % 2
    keep, send, wc, pair = call(
        project_kernel,
        3,
        (shape(80, PIECE), shape(80, PIECE), shape(2048, F), shape(PAIR, F)),
        [
            pltpu.VMEM((1024, F), BF),
            pltpu.VMEM((ROWS, PIECE), F32),
            pltpu.VMEM((32, GW), F32),
            pltpu.VMEM((4 * ROWS, 128), F32),
        ],
        4 * 10**8,
        3 * 10**6,
    )(jnp.stack([me // 4, me % 4, core, source, taking.astype(jnp.int32)]).astype(jnp.int32), x, g, weights)
    swap = [(i, i ^ 1) for i in range(SECT)]
    pieces = (keep.astype(F32) + lax.ppermute(send, "section", swap).astype(F32)).astype(BF)
    share = jnp.concatenate([pieces[64:72, 0:GW], pieces[72:80, 0:GW]], axis=1)
    pieces = jnp.concatenate(
        [pieces[0:64].reshape(8, 8, PIECE), jnp.broadcast_to(share[None], (8, 8, 2 * GW))], axis=2
    )
    total = jnp.sum(exchange(pieces, "section", Y_GROUPS).astype(F32), axis=0)
    share = jnp.concatenate([total[:, PIECE : PIECE + GW], total[:, PIECE + GW :]], axis=0).astype(BF)
    half = exchange(jnp.broadcast_to(share[None], (DP, 16, GW)), "dp")
    other = lax.ppermute(half, "section", swap)

    back = call(
        recur_kernel,
        3,
        shape(8, BACK),
        [
            pltpu.VMEM((1024, GW), BF),
            pltpu.VMEM((16, 3072), F32),
            pltpu.VMEM((16, 1024), BF),
            pltpu.VMEM((16, 1024), F32),
            pltpu.VMEM((16, 1024), F32),
            pltpu.VMEM((16, 1024), F32),
            pltpu.VMEM((16, 1024), F32),
            pltpu.VMEM((8, BACK), F32),
        ],
        2 * 10**8,
        3 * 10**6,
    )(core.reshape(1).astype(jnp.int32), total, half, other)
    back = exchange(jnp.broadcast_to(back[None], (SECT, 8, BACK)), "section")

    keep, send = call(
        grads_kernel,
        4,
        (shape(SECT, 128, 128), shape(SECT, 128, 128)),
        [pltpu.VMEM((SECT, ROWS, F), BF), pltpu.VMEM((1024, ROWS), BF), pltpu.VMEM((1024, ROWS), BF)],
        3 * 10**8,
        3 * 10**6,
    )((me % 2).reshape(1).astype(jnp.int32), x, g, back.reshape(ROWS, BACK), wc)
    grads = scatter_sum(keep, send, me)

    extra_h = back[:, :, 2048:2304].reshape(SECT, 2, 4, 256).transpose(1, 0, 2, 3).reshape(PAIR, 1024)
    own_at = jnp.where(pair_first, PAIR, 0)
    pair_at = jnp.where(pair_first, 0, ROWS)
    rows_out = call(
        rebuild_kernel,
        5,
        shape(SECT, ROWS + PAIR, F),
        [],
        2 * 10**8,
        3 * 10**6,
    )(jnp.stack([own_at, pair_at, alive.astype(jnp.int32)]).astype(jnp.int32), x, pair, back.reshape(ROWS, BACK), extra_h, wc)
    saved = exchange(rows_out, "section")
    saved = call(join_kernel, 1, shape(1, 1, ROWS + PAIR, D), [], 0, 3 * 10**6, False)(saved)

    misc = back[:, :, 2304:2432].astype(F32)
    own_inv = misc[:, :, 16:32] + misc[:, :, 32:48]
    pair_inv = misc[:, 0:2, 48:64] + misc[:, 0:2, 64:80]
    own_inv = lax.dynamic_index_in_dim(own_inv, sec, 2, keepdims=False).reshape(ROWS)
    pair_inv = lax.dynamic_index_in_dim(pair_inv, sec, 2, keepdims=False).T.reshape(PAIR)
    own_inv = jnp.where(alive, own_inv, 0.0)
    pair_inv = jnp.where(taking, pair_inv, 0.0)
    rstd = jnp.where(
        pair_first, jnp.concatenate([pair_inv, own_inv]), jnp.concatenate([own_inv, pair_inv])
    ).reshape(1, 1, ROWS + PAIR)
    return rstd, saved, (grads[64:128] * gain_here)[None], grads[0:64][None]


def solution(mesh):
    in_specs = (
        P("dp", "section"),
        P("dp", "section"),
        P(),
        P("section", None),
        P("section", None, "dp"),
        P("section", None, "dp"),
    )
    out_specs = (
        P("section", "dp", None),
        P("section", "dp", None, None),
        P("section", None, "dp"),
        P("section", None, "dp"),
    )
    return jax.shard_map(body, mesh=mesh, in_specs=in_specs, out_specs=out_specs, check_vma=False)
```

```python
import jax
import jax.numpy as jnp
from jax import lax
from jax.experimental import pallas as pl
from jax.experimental.pallas import tpu as pltpu
from jax.sharding import PartitionSpec as P


EPS = 1e-05
SECT = 16
DP = 32
RANK = 64
D = 4096
F = 256
ROWS = 128
PAIR = 32
PIECE = 3712
BACK = 2432
GW = 1152
F32 = jnp.float32
BF = jnp.bfloat16
NT = (((1,), (1,)), ((), ()))
NN = (((1,), (0,)), ((), ()))
Y_GROUPS = [[2 * y + c for y in range(8)] for c in range(2)]
VMEM_LIMIT = 48 * 1024 * 1024


def dot(a, b, dims):
    return lax.dot_general(a, b, dims, preferred_element_type=F32)


def hi_lo(v):
    hi = v.astype(BF).astype(F32)
    return hi, v - hi


def vmem(n):
    return [pl.BlockSpec(memory_space=pltpu.VMEM)] * n


SMEM = pl.BlockSpec(memory_space=pltpu.SMEM)


def gram_kernel(ints, w_ref, gkeep_ref, gsend_ref, wc_ref, uc_ref, pair_ref, gr_ref):
    p, quarter, core, source = ints[0], ints[1], ints[2], ints[3]
    taking = ints[4] > 0
    for s in range(SECT):
        for h in range(2):
            block = w_ref[2 * (s ^ 8) + h, 0:128, :]
            lanes = slice(128 * h, 128 * h + 128)
            wc_ref[128 * s : 128 * s + 128, lanes] = block
            uc_ref[64 * s : 64 * s + 64, lanes] = block[64:128]
    for h in range(2):
        part = w_ref[source, 128 + 32 * h : 160 + 32 * h, :]
        pair_ref[:, 128 * h : 128 * h + 128] = jnp.where(taking, part, jnp.zeros_like(part))

    m = p // 2 + 1
    small_rows = wc_ref[pl.ds(pl.multiple_of(128 * p + 32 * quarter, 32), 32), :]
    big_rows = wc_ref[pl.ds(pl.multiple_of(128 * (15 - p) + 32 * quarter, 32), 32), :]
    small = dot(small_rows, uc_ref[0:512, :], NT)
    big = dot(big_rows, uc_ref[...], NT)
    st = [small[:, 128 * t : 128 * t + 128] for t in range(4)]
    tiles = [big[:, 128 * t : 128 * t + 128] for t in range(8)]
    tiles.append(st[3])
    for t in range(5, 9):
        for mm in range(1, 5):
            j = t - (9 - mm)
            if 0 <= j < 4:
                tiles[t] = jnp.where(m == mm, st[j], tiles[t])
    for t in range(9):
        gr_ref[:, 128 * t : 128 * t + 128] = tiles[t]
    for gref, part in ((gkeep_ref, core), (gsend_ref, 1 - core)):
        gref[...] = gr_ref[pl.ds(pl.multiple_of(16 * part, 16), 16), :].astype(BF)


def project_kernel(ints, x_ref, pair_ref, g_ref, wc_ref, uc_ref, keep_ref, send_ref, res_ref, ex_ref):
    core, sec = ints[2], ints[5]
    x = x_ref[...]
    pair = pair_ref[...]
    res_ref[:, 0:2048] = dot(x, wc_ref[...], NT)
    res_ref[:, 2048:3072] = dot(g_ref[...], uc_ref[...], NT)
    extra = dot(pair, wc_ref[...], NT)
    for i in range(2):
        for k in range(4):
            for b in range(4):
                at = 512 * k + 128 * b
                ex_ref[pl.ds(128 * b + 4 * i + k, 16, stride=8), :] = extra[16 * i : 16 * i + 16, at : at + 128]
    for b in range(4):
        res_ref[:, 3072 + 128 * b : 3200 + 128 * b] = ex_ref[128 * b : 128 * b + 128, :]

    xf = x.astype(F32)
    pf = pair.astype(F32)
    own_hi, own_lo = hi_lo(jnp.sum(xf * xf, axis=1, keepdims=True))
    pair_hi, pair_lo = hi_lo(jnp.sum(pf * pf, axis=1, keepdims=True))
    ex_ref[0:ROWS, :] = jnp.zeros((ROWS, 128), F32)
    lane = lax.broadcasted_iota(jnp.int32, (PAIR, 128), 1) - 4 * sec
    pair_part = jnp.where(lane == 2, pair_hi, 0.0) + jnp.where(lane == 3, pair_lo, 0.0)
    for i in range(2):
        ex_ref[pl.ds(i, 16, stride=8), :] = pair_part[16 * i : 16 * i + 16]
    lane = lax.broadcasted_iota(jnp.int32, (ROWS, 128), 1) - 4 * sec
    own_part = jnp.where(lane == 0, own_hi, 0.0) + jnp.where(lane == 1, own_lo, 0.0)
    res_ref[:, 3584:3712] = ex_ref[0:ROWS, :] + own_part
    for ref, part in ((keep_ref, core), (send_ref, 1 - core)):
        ref[...] = res_ref[pl.ds(pl.multiple_of(64 * part, 64), 64), :].astype(BF)


def slab_place(s):
    if s >= 8:
        return 15 - s, 0
    return s, 128 * (9 - (s // 2 + 1))


def recur_kernel(ints, sum_ref, mine_ref, other_ref, out_ref, slab_ref, pq_ref, h_ref, acc_ref, t_ref, pre_ref, ds_ref, ho_ref):
    core = ints[0]
    mine_row = pl.multiple_of(16 * core, 16)
    other_row = pl.multiple_of(16 * (1 - core), 16)
    for q in range(DP):
        base = 128 * (q // 4) + 32 * (q % 4)
        slab_ref[pl.ds(base + mine_row, 16), :] = mine_ref[q]
        slab_ref[pl.ds(base + other_row, 16), :] = other_ref[q]
    pq_ref[...] = jnp.zeros_like(pq_ref)
    pq_ref[0:8, :] = sum_ref[:, 0:3072]
    more = sum_ref[:, 3072:3584]
    for i in range(2):
        for k in range(4):
            pq_ref[8 + i : 9 + i, 512 * k : 512 * k + 512] = more[4 * i + k : 4 * i + k + 1]
    h_ref[...] = jnp.zeros_like(h_ref)
    acc_ref[...] = jnp.zeros_like(acc_ref)
    misc = sum_ref[:, 3584:3712]
    pair_lane = lax.broadcasted_iota(jnp.int32, (8, 128), 1) % 4 >= 2
    n_own = jnp.sum(jnp.where(pair_lane, 0.0, misc), axis=1, keepdims=True)
    n_pair = jnp.sum(jnp.where(pair_lane, misc, 0.0), axis=1, keepdims=True)
    n = jnp.concatenate([n_own, n_pair], axis=0)
    row = lax.broadcasted_iota(jnp.int32, (16, 1), 0)
    n = jnp.where(row < 10, n, 0.0)

    inverse = []
    zeros = jnp.zeros((16, RANK), BF)
    for s in range(SECT):
        place, off = slab_place(s)
        r0 = 128 * place
        depth = 128 * ((s + 1) // 2)
        tp = pq_ref[:, 128 * s : 128 * s + 64]
        tq = pq_ref[:, 128 * s + 64 : 128 * s + 128]
        if s:
            before = h_ref[:, 0:depth]
            tp = tp + dot(before, slab_ref[r0 : r0 + 64, off : off + depth], NT)
            tq = tq + dot(before, slab_ref[r0 + 64 : r0 + 128, off : off + depth], NT)
        inv = lax.rsqrt(jnp.maximum(n, 0.0) * (1.0 / D) + EPS)
        inverse.append(inv)
        pre = inv * tp
        sig = 0.5 + 0.5 * jnp.tanh(0.5 * pre)
        hf = pre * sig
        h = hf.astype(BF)
        pre_ref[:, 64 * s : 64 * s + 64] = pre
        ds_ref[:, 64 * s : 64 * s + 64] = sig * (1.0 + pre * (1.0 - sig))
        tile = slice(128 * (s // 2), 128 * (s // 2) + 128)
        own = jnp.concatenate([zeros, h] if s % 2 else [h, zeros], axis=1)
        h_ref[:, tile] = h_ref[:, tile] + own if s % 2 else own
        hd = dot(own, slab_ref[r0 + 64 : r0 + 128, off + tile.start : off + tile.stop], NT)
        n = n + jnp.sum(h.astype(F32) * (2.0 * tq + hd), axis=1, keepdims=True)
        t_ref[:, 64 * s : 64 * s + 64] = tq + hd

    lane16 = lax.broadcasted_iota(jnp.int32, (16, 128), 1)
    beta_sum = jnp.zeros((16, 1), F32)
    misc_out = jnp.zeros((16, 128), F32)
    for s in range(SECT - 1, -1, -1):
        place, off = slab_place(s)
        r0 = 128 * place
        cols = slice(64 * s, 64 * s + 64)
        inv = inverse[s]
        hf = h_ref[:, cols].astype(F32)
        dh = pq_ref[:, 2048 + 64 * s : 2048 + 64 * s + 64] + acc_ref[:, cols] - beta_sum * t_ref[:, cols]
        dp = (dh * ds_ref[:, cols]).astype(BF).astype(F32)
        beta = inv * inv * (jnp.sum(dp * pre_ref[:, cols], axis=1, keepdims=True) * (1.0 / D))
        z = (inv * dp).astype(BF)
        hb = (beta_sum * hf).astype(BF)
        depth = 128 * ((s + 1) // 2)
        for start in range(depth - 128, -1, -128):
            part = slice(start, start + 128)
            acc_ref[:, part] = (
                acc_ref[:, part]
                + dot(z, slab_ref[r0 : r0 + 64, off + start : off + start + 128], NN)
                - dot(hb, slab_ref[r0 + 64 : r0 + 128, off + start : off + start + 128], NN)
            )
        beta_sum = beta_sum + beta
        ho_ref[0:8, 1024 + 64 * s : 1024 + 64 * s + 64] = z[0:8].astype(F32)
        inv_hi, inv_lo = hi_lo(inv)
        misc_out = jnp.where(lane16 == s, beta, misc_out)
        misc_out = jnp.where(lane16 == 16 + s, inv_hi, misc_out)
        misc_out = jnp.where(lane16 == 32 + s, inv_lo, misc_out)
    h_all = h_ref[...].astype(F32)
    ho_ref[0:8, 0:1024] = h_all[0:8]
    for i in range(2):
        for k in range(4):
            ho_ref[4 * i + k : 4 * i + k + 1, 2048:2304] = h_all[8 + i : 9 + i, 256 * k : 256 * k + 256]
    extra_misc = pltpu.roll(misc_out[8:16], 32, 1)
    lane8 = lax.broadcasted_iota(jnp.int32, (8, 128), 1)
    row8 = lax.broadcasted_iota(jnp.int32, (8, 128), 0)
    keep = (lane8 >= 48) & (lane8 < 80) & (row8 < 2)
    ho_ref[0:8, 2304:2432] = jnp.where(keep, extra_misc, jnp.where(lane8 < 48, misc_out[0:8], 0.0))
    out_ref[...] = ho_ref[...].astype(BF)


def rebuild_kernel(ints, x_ref, pair_ref, mine_ref, other_ref, eh_ref, wc_ref, out_ref, back_ref):
    gather_rows(ints[3], mine_ref, other_ref, back_ref)
    own_at = pl.multiple_of(ints[0], 32)
    pair_at = pl.multiple_of(ints[1], 32)
    alive = ints[2] > 0
    x = x_ref[...].astype(F32)
    e = pair_ref[...].astype(F32)
    for s in range(SECT):
        out_ref[s, pl.ds(own_at, ROWS), :] = jnp.where(alive, x, 0.0).astype(BF)
        out_ref[s, pl.ds(pair_at, PAIR), :] = e.astype(BF)
        if s < SECT - 1:
            up = wc_ref[128 * s + 64 : 128 * s + 128, :]
            x = x + dot(back_ref[:, 64 * s : 64 * s + 64], up, NN)
            e = e + dot(eh_ref[:, 64 * s : 64 * s + 64], up, NN)


def gather_rows(core, mine_ref, other_ref, full_ref):
    full_ref[pl.ds(pl.multiple_of(64 * core, 64), 64), :] = mine_ref[...]
    full_ref[pl.ds(pl.multiple_of(64 * (1 - core), 64), 64), :] = other_ref[...]


def pick(values, index):
    out = values[0]
    for k in range(1, len(values)):
        out = jnp.where(index == k, values[k], out)
    return out


def grads_kernel(ints, x_ref, g_ref, mine_ref, other_ref, wc_ref, o0, o1, o2, o3, back_ref, xs_ref, ht_ref, zt_ref):
    gather_rows(ints[0], mine_ref, other_ref, back_ref)
    along = ints[1]
    ht_ref[...] = back_ref[:, 0:1024].T
    zt_ref[...] = back_ref[:, 1024:2048].T
    x = x_ref[...].astype(F32)
    for s in range(SECT):
        xs_ref[s] = x.astype(BF)
        if s < SECT - 1:
            x = x + dot(back_ref[:, 64 * s : 64 * s + 64], wc_ref[128 * s + 64 : 128 * s + 128, :], NN)
    g = g_ref[...].astype(F32)
    betas = back_ref[:, 2304:2432].astype(F32)
    blocks = [None] * 4
    for s in range(SECT - 1, -1, -1):
        xs = xs_ref[s]
        up = dot(ht_ref[64 * s : 64 * s + 64, :], g.astype(BF), NN)
        down = dot(zt_ref[64 * s : 64 * s + 64, :], xs, NN)
        both = jnp.concatenate([up, down], axis=0).astype(BF)
        for h in range(2):
            blocks[2 * (s % 2) + h] = both[:, 128 * h : 128 * h + 128]
        if s % 2 == 0:
            for k, ref in enumerate((o0, o1, o2, o3)):
                ref[s // 2 ^ 4] = pick(blocks, along ^ k)
        if s:
            z = back_ref[:, 1024 + 64 * s : 1024 + 64 * s + 64]
            g = g + dot(z, wc_ref[128 * s : 128 * s + 64, :], NN) - betas[:, s : s + 1] * xs.astype(F32)


def join_kernel(in_ref, out_ref):
    for k in range(SECT):
        out_ref[0, 0, :, F * k : F * k + F] = in_ref[k]


def call(kernel, n_in, outs, scratch, flops, nbytes, with_ints=True):
    return pl.pallas_call(
        kernel,
        out_shape=outs,
        in_specs=([SMEM] if with_ints else []) + vmem(n_in),
        out_specs=jax.tree.map(lambda _: pl.BlockSpec(memory_space=pltpu.VMEM), outs),
        scratch_shapes=scratch,
        compiler_params=pltpu.CompilerParams(vmem_limit_bytes=VMEM_LIMIT),
        cost_estimate=pl.CostEstimate(flops=flops, bytes_accessed=nbytes, transcendentals=0),
    )


def shape(*dims, kind=BF):
    return jax.ShapeDtypeStruct(dims, kind)


def exchange(value, axis, groups=None):
    return lax.all_to_all(value, axis, 0, 0, tiled=True, axis_index_groups=groups)


def flip(value, bits):
    return lax.ppermute(value, "dp", [(i, i ^ bits) for i in range(DP)])


def scatter_sum(own, arrived, me):
    value = own.astype(F32)
    for part in arrived:
        value = value + part.astype(F32)
    for b in (2, 4, 3):
        blocks = value.astype(BF).reshape((-1, 2, 128, 128))
        if b == 4:
            blocks = blocks.reshape(2, 2, 128, 128).swapaxes(0, 1)
        bit = (me >> b) & 1
        keep = lax.dynamic_index_in_dim(blocks, bit, 1, keepdims=False)
        send = lax.dynamic_index_in_dim(blocks, 1 - bit, 1, keepdims=False)
        if b != 3:
            value = keep.astype(F32) + flip(send, 1 << b).astype(F32)
    both = ("section", "dp")
    mine = lax.ppermute(keep[0], both, [(a, owner(a // DP, a % DP)) for a in range(SECT * DP)])
    theirs = lax.ppermute(send[0], both, [(a, owner(a // DP, a % DP ^ 8)) for a in range(SECT * DP)])
    return mine.astype(F32) + theirs.astype(F32)


def owner(sec, q):
    return (q // 2 ^ 8) * DP + 2 * sec + q % 2


def body(x, g, worker, gain, narrow, widen):
    sec = lax.axis_index("section")
    me = lax.axis_index("dp")

    gain_here = lax.dynamic_slice(gain, (0, 128 * me), (1, 128))
    block = jnp.concatenate([(narrow[0].astype(F32) * gain_here).astype(BF), widen[0]], axis=0)
    block = lax.ppermute(block, ("section", "dp"), [(owner(a // DP, a % DP), a) for a in range(SECT * DP)])

    owners = jnp.arange(DP, dtype=jnp.int32)
    takers = worker[:, ::2]
    mine = lax.dynamic_index_in_dim(takers, me, 0, keepdims=False)
    alive = mine[0] == me
    comes = jnp.any((takers == me) & (owners != me)[:, None], axis=1)
    source = jnp.sum(jnp.where(comes, owners, 0))
    taking = jnp.any(comes)
    pair_first = taking & (source < me)
    goes = (mine[None, :] == owners[:, None]) & jnp.logical_not(alive)
    quads = jnp.concatenate([x[:, 0:128].reshape(4, PAIR, 128), x[:, 128:256].reshape(4, PAIR, 128)], axis=1)
    outgoing = jnp.zeros((DP, 2 * PAIR, 128), BF)
    for j in range(4):
        outgoing = jnp.where(goes[:, j][:, None, None], quads[j][None], outgoing)
    weights = jnp.concatenate([jnp.broadcast_to(block[None], (DP, 128, 128)), outgoing], axis=1)
    weights = exchange(weights, "dp")

    core = sec % 2
    ints = jnp.stack([me // 4, me % 4, core, source, taking.astype(jnp.int32), sec]).astype(jnp.int32)
    gkeep, gsend, wc, uc, pair = call(
        gram_kernel,
        1,
        (shape(16, GW), shape(16, GW), shape(2048, F), shape(1024, F), shape(PAIR, F)),
        [pltpu.VMEM((32, GW), F32)],
        10**8,
        3 * 10**6,
    )(ints, weights)
    swap = [(i, i ^ 1) for i in range(SECT)]
    share = (gkeep.astype(F32) + lax.ppermute(gsend, "section", swap).astype(F32)).astype(BF)
    keep, send = call(
        project_kernel,
        5,
        (shape(64, PIECE), shape(64, PIECE)),
        [pltpu.VMEM((ROWS, PIECE), F32), pltpu.VMEM((4 * ROWS, 128), F32)],
        3 * 10**8,
        3 * 10**6,
    )(ints, x, pair, g, wc, uc)
    share = exchange(jnp.broadcast_to(share[None], (8, 16, GW)), "section", Y_GROUPS)
    share = jnp.sum(share.astype(F32), axis=0).astype(BF)
    half = exchange(jnp.broadcast_to(share[None], (DP, 16, GW)), "dp")

    rows = (keep.astype(F32) + lax.ppermute(send, "section", swap).astype(F32)).astype(BF).reshape(8, 8, PIECE)
    bit = (sec >> 1) & 1
    both = rows.reshape(4, 2, 8, PIECE)
    send = lax.dynamic_index_in_dim(both, 1 - bit, 1, keepdims=False)
    send = lax.ppermute(send, "section", [(i, i ^ 2) for i in range(SECT)])
    rows = (lax.dynamic_index_in_dim(both, bit, 1, keepdims=False).astype(F32) + send.astype(F32)).astype(BF)
    here = sec // 4
    total = lax.dynamic_index_in_dim(rows, here, 0, keepdims=False).astype(F32)
    for k in range(1, 4):
        send = lax.dynamic_index_in_dim(rows, here ^ k, 0, keepdims=False)
        total = total + lax.ppermute(send, "section", [(i, i ^ (4 * k)) for i in range(SECT)]).astype(F32)
    half, total = lax.optimization_barrier((half, total))
    other = lax.ppermute(half, "section", swap)

    back = call(
        recur_kernel,
        3,
        shape(8, BACK),
        [
            pltpu.VMEM((1024, GW), BF),
            pltpu.VMEM((16, 3072), F32),
            pltpu.VMEM((16, 1024), BF),
            pltpu.VMEM((16, 1024), F32),
            pltpu.VMEM((16, 1024), F32),
            pltpu.VMEM((16, 1024), F32),
            pltpu.VMEM((16, 1024), F32),
            pltpu.VMEM((8, BACK), F32),
        ],
        2 * 10**8,
        3 * 10**6,
    )(core.reshape(1).astype(jnp.int32), total, half, other)
    back = exchange(jnp.broadcast_to(back[None], (8, 8, BACK)), "section", Y_GROUPS).reshape(64, BACK)
    back_other = lax.ppermute(back, "section", swap)

    blocks = call(
        grads_kernel,
        5,
        (shape(8, 128, 128),) * 4,
        [
            pltpu.VMEM((ROWS, BACK), BF),
            pltpu.VMEM((SECT, ROWS, F), BF),
            pltpu.VMEM((1024, ROWS), BF),
            pltpu.VMEM((1024, ROWS), BF),
        ],
        3 * 10**8,
        3 * 10**6,
    )(jnp.stack([core, me % 4]).astype(jnp.int32), x, g, back, back_other, wc)
    arrived = [flip(blocks[k], k) for k in (1, 3, 2)]

    small, small_other = back[:, 2048:2432], back_other[:, 2048:2432]
    small = jnp.where(
        core == 0, jnp.concatenate([small, small_other], axis=0), jnp.concatenate([small_other, small], axis=0)
    ).reshape(SECT, 8, 384)
    extra_h = small[:, :, 0:256].reshape(SECT, 2, 4, 256).transpose(1, 0, 2, 3).reshape(PAIR, 1024)
    own_at = jnp.where(pair_first, PAIR, 0)
    pair_at = jnp.where(pair_first, 0, ROWS)
    rows_out = call(
        rebuild_kernel,
        6,
        shape(SECT, ROWS + PAIR, F),
        [pltpu.VMEM((ROWS, BACK), BF)],
        2 * 10**8,
        3 * 10**6,
    )(jnp.stack([own_at, pair_at, alive.astype(jnp.int32), core]).astype(jnp.int32), x, pair, back, back_other, extra_h, wc)
    saved = exchange(rows_out, "section")
    grads = scatter_sum(blocks[0], arrived, me)
    saved = call(join_kernel, 1, shape(1, 1, ROWS + PAIR, D), [], 0, 3 * 10**6, False)(saved)

    misc = small[:, :, 256:384].astype(F32)
    own_inv = misc[:, :, 16:32] + misc[:, :, 32:48]
    pair_inv = misc[:, 0:2, 48:64] + misc[:, 0:2, 64:80]
    own_inv = lax.dynamic_index_in_dim(own_inv, sec, 2, keepdims=False).reshape(ROWS)
    pair_inv = lax.dynamic_index_in_dim(pair_inv, sec, 2, keepdims=False).T.reshape(PAIR)
    own_inv = jnp.where(alive, own_inv, 0.0)
    pair_inv = jnp.where(taking, pair_inv, 0.0)
    rstd = jnp.where(
        pair_first, jnp.concatenate([pair_inv, own_inv]), jnp.concatenate([own_inv, pair_inv])
    ).reshape(1, 1, ROWS + PAIR)
    return rstd, saved, (grads[64:128] * gain_here)[None], grads[0:64][None]


def solution(mesh):
    in_specs = (
        P("dp", "section"),
        P("dp", "section"),
        P(),
        P("section", None),
        P("section", None, "dp"),
        P("section", None, "dp"),
    )
    out_specs = (
        P("section", "dp", None),
        P("section", "dp", None, None),
        P("section", None, "dp"),
        P("section", None, "dp"),
    )
    return jax.shard_map(body, mesh=mesh, in_specs=in_specs, out_specs=out_specs, check_vma=False)
```

```python
import jax
import jax.numpy as jnp
from jax import lax
from jax.experimental import pallas as pl
from jax.experimental.pallas import tpu as pltpu
from jax.sharding import PartitionSpec as P


EPS = 1e-05
SECT = 16
DP = 32
RANK = 64
D = 4096
F = 256
ROWS = 128
PAIR = 32
PIECE = 3712
BACK = 2432
GW = 1152
F32 = jnp.float32
BF = jnp.bfloat16
NT = (((1,), (1,)), ((), ()))
NN = (((1,), (0,)), ((), ()))
Y_GROUPS = [[2 * y + c for y in range(8)] for c in range(2)]
VMEM_LIMIT = 48 * 1024 * 1024


def dot(a, b, dims):
    return lax.dot_general(a, b, dims, preferred_element_type=F32)


def hi_lo(v):
    hi = v.astype(BF).astype(F32)
    return hi, v - hi


def vmem(n):
    return [pl.BlockSpec(memory_space=pltpu.VMEM)] * n


SMEM = pl.BlockSpec(memory_space=pltpu.SMEM)


def gram_kernel(ints, w_ref, gkeep_ref, gsend_ref, wc_ref, uc_ref, pair_ref, gr_ref):
    p, quarter, core, source = ints[0], ints[1], ints[2], ints[3]
    taking = ints[4] > 0
    for s in range(SECT):
        for h in range(2):
            block = w_ref[2 * (s ^ 8) + h, 0:128, :]
            lanes = slice(128 * h, 128 * h + 128)
            wc_ref[128 * s : 128 * s + 128, lanes] = block
            uc_ref[64 * s : 64 * s + 64, lanes] = block[64:128]
    for h in range(2):
        part = w_ref[source, 128 + 32 * h : 160 + 32 * h, :]
        pair_ref[:, 128 * h : 128 * h + 128] = jnp.where(taking, part, jnp.zeros_like(part))

    m = p // 2 + 1
    small_rows = wc_ref[pl.ds(pl.multiple_of(128 * p + 32 * quarter, 32), 32), :]
    big_rows = wc_ref[pl.ds(pl.multiple_of(128 * (15 - p) + 32 * quarter, 32), 32), :]
    small = dot(small_rows, uc_ref[0:512, :], NT)
    big = dot(big_rows, uc_ref[...], NT)
    st = [small[:, 128 * t : 128 * t + 128] for t in range(4)]
    tiles = [big[:, 128 * t : 128 * t + 128] for t in range(8)]
    tiles.append(st[3])
    for t in range(5, 9):
        for mm in range(1, 5):
            j = t - (9 - mm)
            if 0 <= j < 4:
                tiles[t] = jnp.where(m == mm, st[j], tiles[t])
    for t in range(9):
        gr_ref[:, 128 * t : 128 * t + 128] = tiles[t]
    for gref, part in ((gkeep_ref, core), (gsend_ref, 1 - core)):
        gref[...] = gr_ref[pl.ds(pl.multiple_of(16 * part, 16), 16), :].astype(BF)


def project_kernel(ints, x_ref, pair_ref, g_ref, wc_ref, uc_ref, keep_ref, send_ref, res_ref, ex_ref):
    core, sec = ints[2], ints[5]
    x = x_ref[...]
    pair = pair_ref[...]
    res_ref[:, 0:2048] = dot(x, wc_ref[...], NT)
    res_ref[:, 2048:3072] = dot(g_ref[...], uc_ref[...], NT)
    extra = dot(pair, wc_ref[...], NT)
    for i in range(2):
        for k in range(4):
            for b in range(4):
                at = 512 * k + 128 * b
                ex_ref[pl.ds(128 * b + 4 * i + k, 16, stride=8), :] = extra[16 * i : 16 * i + 16, at : at + 128]
    for b in range(4):
        res_ref[:, 3072 + 128 * b : 3200 + 128 * b] = ex_ref[128 * b : 128 * b + 128, :]

    xf = x.astype(F32)
    pf = pair.astype(F32)
    own_hi, own_lo = hi_lo(jnp.sum(xf * xf, axis=1, keepdims=True))
    pair_hi, pair_lo = hi_lo(jnp.sum(pf * pf, axis=1, keepdims=True))
    ex_ref[0:ROWS, :] = jnp.zeros((ROWS, 128), F32)
    lane = lax.broadcasted_iota(jnp.int32, (PAIR, 128), 1) - 4 * sec
    pair_part = jnp.where(lane == 2, pair_hi, 0.0) + jnp.where(lane == 3, pair_lo, 0.0)
    for i in range(2):
        ex_ref[pl.ds(i, 16, stride=8), :] = pair_part[16 * i : 16 * i + 16]
    lane = lax.broadcasted_iota(jnp.int32, (ROWS, 128), 1) - 4 * sec
    own_part = jnp.where(lane == 0, own_hi, 0.0) + jnp.where(lane == 1, own_lo, 0.0)
    res_ref[:, 3584:3712] = ex_ref[0:ROWS, :] + own_part
    for ref, part in ((keep_ref, core), (send_ref, 1 - core)):
        ref[...] = res_ref[pl.ds(pl.multiple_of(64 * part, 64), 64), :].astype(BF)


def slab_place(s):
    if s >= 8:
        return 15 - s, 0
    return s, 128 * (9 - (s // 2 + 1))


def recur_kernel(ints, sum_ref, mine_ref, other_ref, out_ref, slab_ref, pq_ref, h_ref, acc_ref, t_ref, pre_ref, ds_ref, ho_ref):
    core = ints[0]
    mine_row = pl.multiple_of(16 * core, 16)
    other_row = pl.multiple_of(16 * (1 - core), 16)
    for q in range(DP):
        base = 128 * (q // 4) + 32 * (q % 4)
        slab_ref[pl.ds(base + mine_row, 16), :] = mine_ref[q]
        slab_ref[pl.ds(base + other_row, 16), :] = other_ref[q]
    pq_ref[...] = jnp.zeros_like(pq_ref)
    pq_ref[0:8, :] = sum_ref[:, 0:3072]
    more = sum_ref[:, 3072:3584]
    for i in range(2):
        for k in range(4):
            pq_ref[8 + i : 9 + i, 512 * k : 512 * k + 512] = more[4 * i + k : 4 * i + k + 1]
    h_ref[...] = jnp.zeros_like(h_ref)
    acc_ref[...] = jnp.zeros_like(acc_ref)
    misc = sum_ref[:, 3584:3712]
    pair_lane = lax.broadcasted_iota(jnp.int32, (8, 128), 1) % 4 >= 2
    n_own = jnp.sum(jnp.where(pair_lane, 0.0, misc), axis=1, keepdims=True)
    n_pair = jnp.sum(jnp.where(pair_lane, misc, 0.0), axis=1, keepdims=True)
    n = jnp.concatenate([n_own, n_pair], axis=0)
    row = lax.broadcasted_iota(jnp.int32, (16, 1), 0)
    n = jnp.where(row < 10, n, 0.0)

    inverse = []
    zeros = jnp.zeros((16, RANK), BF)
    for s in range(SECT):
        place, off = slab_place(s)
        r0 = 128 * place
        depth = 128 * ((s + 1) // 2)
        tp = pq_ref[:, 128 * s : 128 * s + 64]
        tq = pq_ref[:, 128 * s + 64 : 128 * s + 128]
        if s:
            before = h_ref[:, 0:depth]
            tp = tp + dot(before, slab_ref[r0 : r0 + 64, off : off + depth], NT)
            tq = tq + dot(before, slab_ref[r0 + 64 : r0 + 128, off : off + depth], NT)
        inv = lax.rsqrt(jnp.maximum(n, 0.0) * (1.0 / D) + EPS)
        inverse.append(inv)
        pre = inv * tp
        sig = 0.5 + 0.5 * jnp.tanh(0.5 * pre)
        hf = pre * sig
        h = hf.astype(BF)
        pre_ref[:, 64 * s : 64 * s + 64] = pre
        ds_ref[:, 64 * s : 64 * s + 64] = sig * (1.0 + pre * (1.0 - sig))
        tile = slice(128 * (s // 2), 128 * (s // 2) + 128)
        own = jnp.concatenate([zeros, h] if s % 2 else [h, zeros], axis=1)
        h_ref[:, tile] = h_ref[:, tile] + own if s % 2 else own
        hd = dot(own, slab_ref[r0 + 64 : r0 + 128, off + tile.start : off + tile.stop], NT)
        n = n + jnp.sum(h.astype(F32) * (2.0 * tq + hd), axis=1, keepdims=True)
        t_ref[:, 64 * s : 64 * s + 64] = tq + hd

    lane16 = lax.broadcasted_iota(jnp.int32, (16, 128), 1)
    beta_sum = jnp.zeros((16, 1), F32)
    misc_out = jnp.zeros((16, 128), F32)
    for s in range(SECT - 1, -1, -1):
        place, off = slab_place(s)
        r0 = 128 * place
        cols = slice(64 * s, 64 * s + 64)
        inv = inverse[s]
        hf = h_ref[:, cols].astype(F32)
        dh = pq_ref[:, 2048 + 64 * s : 2048 + 64 * s + 64] + acc_ref[:, cols] - beta_sum * t_ref[:, cols]
        dp = (dh * ds_ref[:, cols]).astype(BF).astype(F32)
        beta = inv * inv * (jnp.sum(dp * pre_ref[:, cols], axis=1, keepdims=True) * (1.0 / D))
        z = (inv * dp).astype(BF)
        hb = (beta_sum * hf).astype(BF)
        depth = 128 * ((s + 1) // 2)
        for start in range(depth - 128, -1, -128):
            part = slice(start, start + 128)
            acc_ref[:, part] = (
                acc_ref[:, part]
                + dot(z, slab_ref[r0 : r0 + 64, off + start : off + start + 128], NN)
                - dot(hb, slab_ref[r0 + 64 : r0 + 128, off + start : off + start + 128], NN)
            )
        beta_sum = beta_sum + beta
        ho_ref[0:8, 1024 + 64 * s : 1024 + 64 * s + 64] = z[0:8].astype(F32)
        inv_hi, inv_lo = hi_lo(inv)
        misc_out = jnp.where(lane16 == s, beta, misc_out)
        misc_out = jnp.where(lane16 == 16 + s, inv_hi, misc_out)
        misc_out = jnp.where(lane16 == 32 + s, inv_lo, misc_out)
    h_all = h_ref[...].astype(F32)
    ho_ref[0:8, 0:1024] = h_all[0:8]
    for i in range(2):
        for k in range(4):
            ho_ref[4 * i + k : 4 * i + k + 1, 2048:2304] = h_all[8 + i : 9 + i, 256 * k : 256 * k + 256]
    extra_misc = pltpu.roll(misc_out[8:16], 32, 1)
    lane8 = lax.broadcasted_iota(jnp.int32, (8, 128), 1)
    row8 = lax.broadcasted_iota(jnp.int32, (8, 128), 0)
    keep = (lane8 >= 48) & (lane8 < 80) & (row8 < 2)
    ho_ref[0:8, 2304:2432] = jnp.where(keep, extra_misc, jnp.where(lane8 < 48, misc_out[0:8], 0.0))
    out_ref[...] = ho_ref[...].astype(BF)


def rebuild_kernel(ints, x_ref, pair_ref, mine_ref, other_ref, eh_ref, wc_ref, out_ref, back_ref):
    gather_rows(ints[3], mine_ref, other_ref, back_ref)
    own_at = pl.multiple_of(ints[0], 32)
    pair_at = pl.multiple_of(ints[1], 32)
    alive = ints[2] > 0
    x = x_ref[...].astype(F32)
    e = pair_ref[...].astype(F32)
    for s in range(SECT):
        out_ref[s, pl.ds(own_at, ROWS), :] = jnp.where(alive, x, 0.0).astype(BF)
        out_ref[s, pl.ds(pair_at, PAIR), :] = e.astype(BF)
        if s < SECT - 1:
            up = wc_ref[128 * s + 64 : 128 * s + 128, :]
            x = x + dot(back_ref[:, 64 * s : 64 * s + 64], up, NN)
            e = e + dot(eh_ref[:, 64 * s : 64 * s + 64], up, NN)


def gather_rows(core, mine_ref, other_ref, full_ref):
    full_ref[pl.ds(pl.multiple_of(64 * core, 64), 64), :] = mine_ref[...]
    full_ref[pl.ds(pl.multiple_of(64 * (1 - core), 64), 64), :] = other_ref[...]


def pick(values, index):
    out = values[0]
    for k in range(1, len(values)):
        out = jnp.where(index == k, values[k], out)
    return out


def grads_kernel(ints, x_ref, g_ref, mine_ref, other_ref, wc_ref, keep_ref, send_ref, back_ref, xs_ref, ht_ref, zt_ref):
    gather_rows(ints[0], mine_ref, other_ref, back_ref)
    along = ints[1]
    ht_ref[...] = back_ref[:, 0:1024].T
    zt_ref[...] = back_ref[:, 1024:2048].T
    x = x_ref[...].astype(F32)
    for s in range(SECT):
        xs_ref[s] = x.astype(BF)
        if s < SECT - 1:
            x = x + dot(back_ref[:, 64 * s : 64 * s + 64], wc_ref[128 * s + 64 : 128 * s + 128, :], NN)
    g = g_ref[...].astype(F32)
    betas = back_ref[:, 2304:2432].astype(F32)
    blocks = [None] * 4
    for s in range(SECT - 1, -1, -1):
        xs = xs_ref[s]
        up = dot(ht_ref[64 * s : 64 * s + 64, :], g.astype(BF), NN)
        down = dot(zt_ref[64 * s : 64 * s + 64, :], xs, NN)
        both = jnp.concatenate([up, down], axis=0).astype(BF)
        for h in range(2):
            blocks[2 * (s % 2) + h] = both[:, 128 * h : 128 * h + 128]
        if s % 2 == 0:
            for ref, flips in ((keep_ref, (0, 3)), (send_ref, (1, 2))):
                for k in range(2):
                    ref[k, s // 2 ^ 4] = pick(blocks, along ^ flips[k])
        if s:
            z = back_ref[:, 1024 + 64 * s : 1024 + 64 * s + 64]
            g = g + dot(z, wc_ref[128 * s : 128 * s + 64, :], NN) - betas[:, s : s + 1] * xs.astype(F32)


def join_kernel(in_ref, out_ref):
    for k in range(SECT):
        out_ref[0, 0, :, F * k : F * k + F] = in_ref[k]


def call(kernel, n_in, outs, scratch, flops, nbytes, with_ints=True):
    return pl.pallas_call(
        kernel,
        out_shape=outs,
        in_specs=([SMEM] if with_ints else []) + vmem(n_in),
        out_specs=jax.tree.map(lambda _: pl.BlockSpec(memory_space=pltpu.VMEM), outs),
        scratch_shapes=scratch,
        compiler_params=pltpu.CompilerParams(vmem_limit_bytes=VMEM_LIMIT),
        cost_estimate=pl.CostEstimate(flops=flops, bytes_accessed=nbytes, transcendentals=0),
    )


def shape(*dims, kind=BF):
    return jax.ShapeDtypeStruct(dims, kind)


def exchange(value, axis, groups=None):
    return lax.all_to_all(value, axis, 0, 0, tiled=True, axis_index_groups=groups)


def flip(value, bits):
    return lax.ppermute(value, "dp", [(i, i ^ bits) for i in range(DP)])


def scatter_sum(keep, send, me):
    value = keep.astype(F32) + flip(send, 1).astype(F32)
    value = value[0] + flip(value[1].astype(BF), 3).astype(F32)
    for b in (2, 4, 3):
        blocks = value.astype(BF).reshape((-1, 2, 128, 128))
        if b == 4:
            blocks = blocks.reshape(2, 2, 128, 128).swapaxes(0, 1)
        bit = (me >> b) & 1
        keep = lax.dynamic_index_in_dim(blocks, bit, 1, keepdims=False)
        send = lax.dynamic_index_in_dim(blocks, 1 - bit, 1, keepdims=False)
        if b != 3:
            value = keep.astype(F32) + flip(send, 1 << b).astype(F32)
    both = ("section", "dp")
    mine = lax.ppermute(keep[0], both, [(a, owner(a // DP, a % DP)) for a in range(SECT * DP)])
    theirs = lax.ppermute(send[0], both, [(a, owner(a // DP, a % DP ^ 8)) for a in range(SECT * DP)])
    return mine.astype(F32) + theirs.astype(F32)


def owner(sec, q):
    return (q // 2 ^ 8) * DP + 2 * sec + q % 2


def body(x, g, worker, gain, narrow, widen):
    sec = lax.axis_index("section")
    me = lax.axis_index("dp")

    gain_here = lax.dynamic_slice(gain, (0, 128 * me), (1, 128))
    block = jnp.concatenate([(narrow[0].astype(F32) * gain_here).astype(BF), widen[0]], axis=0)
    block = lax.ppermute(block, ("section", "dp"), [(owner(a // DP, a % DP), a) for a in range(SECT * DP)])

    owners = jnp.arange(DP, dtype=jnp.int32)
    takers = worker[:, ::2]
    mine = lax.dynamic_index_in_dim(takers, me, 0, keepdims=False)
    alive = mine[0] == me
    comes = jnp.any((takers == me) & (owners != me)[:, None], axis=1)
    source = jnp.sum(jnp.where(comes, owners, 0))
    taking = jnp.any(comes)
    pair_first = taking & (source < me)
    goes = (mine[None, :] == owners[:, None]) & jnp.logical_not(alive)
    quads = jnp.concatenate([x[:, 0:128].reshape(4, PAIR, 128), x[:, 128:256].reshape(4, PAIR, 128)], axis=1)
    outgoing = jnp.zeros((DP, 2 * PAIR, 128), BF)
    for j in range(4):
        outgoing = jnp.where(goes[:, j][:, None, None], quads[j][None], outgoing)
    weights = jnp.concatenate([jnp.broadcast_to(block[None], (DP, 128, 128)), outgoing], axis=1)
    weights = exchange(weights, "dp")

    core = sec % 2
    ints = jnp.stack([me // 4, me % 4, core, source, taking.astype(jnp.int32), sec]).astype(jnp.int32)
    gkeep, gsend, wc, uc, pair = call(
        gram_kernel,
        1,
        (shape(16, GW), shape(16, GW), shape(2048, F), shape(1024, F), shape(PAIR, F)),
        [pltpu.VMEM((32, GW), F32)],
        10**8,
        3 * 10**6,
    )(ints, weights)
    swap = [(i, i ^ 1) for i in range(SECT)]
    share = (gkeep.astype(F32) + lax.ppermute(gsend, "section", swap).astype(F32)).astype(BF)
    keep, send = call(
        project_kernel,
        5,
        (shape(64, PIECE), shape(64, PIECE)),
        [pltpu.VMEM((ROWS, PIECE), F32), pltpu.VMEM((4 * ROWS, 128), F32)],
        3 * 10**8,
        3 * 10**6,
    )(ints, x, pair, g, wc, uc)
    share = exchange(jnp.broadcast_to(share[None], (8, 16, GW)), "section", Y_GROUPS)
    share = jnp.sum(share.astype(F32), axis=0).astype(BF)
    half = exchange(jnp.broadcast_to(share[None], (DP, 16, GW)), "dp")

    rows = (keep.astype(F32) + lax.ppermute(send, "section", swap).astype(F32)).astype(BF).reshape(8, 8, PIECE)
    bit = (sec >> 1) & 1
    both = rows.reshape(4, 2, 8, PIECE)
    send = lax.dynamic_index_in_dim(both, 1 - bit, 1, keepdims=False)
    send = lax.ppermute(send, "section", [(i, i ^ 2) for i in range(SECT)])
    rows = (lax.dynamic_index_in_dim(both, bit, 1, keepdims=False).astype(F32) + send.astype(F32)).astype(BF)
    here = sec // 4
    total = lax.dynamic_index_in_dim(rows, here, 0, keepdims=False).astype(F32)
    for k in range(1, 4):
        send = lax.dynamic_index_in_dim(rows, here ^ k, 0, keepdims=False)
        total = total + lax.ppermute(send, "section", [(i, i ^ (4 * k)) for i in range(SECT)]).astype(F32)
    half, total = lax.optimization_barrier((half, total))
    other = lax.ppermute(half, "section", swap)

    back = call(
        recur_kernel,
        3,
        shape(8, BACK),
        [
            pltpu.VMEM((1024, GW), BF),
            pltpu.VMEM((16, 3072), F32),
            pltpu.VMEM((16, 1024), BF),
            pltpu.VMEM((16, 1024), F32),
            pltpu.VMEM((16, 1024), F32),
            pltpu.VMEM((16, 1024), F32),
            pltpu.VMEM((16, 1024), F32),
            pltpu.VMEM((8, BACK), F32),
        ],
        2 * 10**8,
        3 * 10**6,
    )(core.reshape(1).astype(jnp.int32), total, half, other)
    back = exchange(jnp.broadcast_to(back[None], (8, 8, BACK)), "section", Y_GROUPS).reshape(64, BACK)
    back_other = lax.ppermute(back, "section", swap)

    blocks = call(
        grads_kernel,
        5,
        (shape(2, 8, 128, 128),) * 2,
        [
            pltpu.VMEM((ROWS, BACK), BF),
            pltpu.VMEM((SECT, ROWS, F), BF),
            pltpu.VMEM((1024, ROWS), BF),
            pltpu.VMEM((1024, ROWS), BF),
        ],
        3 * 10**8,
        3 * 10**6,
    )(jnp.stack([core, me % 4]).astype(jnp.int32), x, g, back, back_other, wc)

    small, small_other = back[:, 2048:2432], back_other[:, 2048:2432]
    small = jnp.where(
        core == 0, jnp.concatenate([small, small_other], axis=0), jnp.concatenate([small_other, small], axis=0)
    ).reshape(SECT, 8, 384)
    extra_h = small[:, :, 0:256].reshape(SECT, 2, 4, 256).transpose(1, 0, 2, 3).reshape(PAIR, 1024)
    own_at = jnp.where(pair_first, PAIR, 0)
    pair_at = jnp.where(pair_first, 0, ROWS)
    rows_out = call(
        rebuild_kernel,
        6,
        shape(SECT, ROWS + PAIR, F),
        [pltpu.VMEM((ROWS, BACK), BF)],
        2 * 10**8,
        3 * 10**6,
    )(jnp.stack([own_at, pair_at, alive.astype(jnp.int32), core]).astype(jnp.int32), x, pair, back, back_other, extra_h, wc)
    saved = exchange(rows_out, "section")
    grads = scatter_sum(*blocks, me)
    saved = call(join_kernel, 1, shape(1, 1, ROWS + PAIR, D), [], 0, 3 * 10**6, False)(saved)

    misc = small[:, :, 256:384].astype(F32)
    own_inv = misc[:, :, 16:32] + misc[:, :, 32:48]
    pair_inv = misc[:, 0:2, 48:64] + misc[:, 0:2, 64:80]
    own_inv = lax.dynamic_index_in_dim(own_inv, sec, 2, keepdims=False).reshape(ROWS)
    pair_inv = lax.dynamic_index_in_dim(pair_inv, sec, 2, keepdims=False).T.reshape(PAIR)
    own_inv = jnp.where(alive, own_inv, 0.0)
    pair_inv = jnp.where(taking, pair_inv, 0.0)
    rstd = jnp.where(
        pair_first, jnp.concatenate([pair_inv, own_inv]), jnp.concatenate([own_inv, pair_inv])
    ).reshape(1, 1, ROWS + PAIR)
    return rstd, saved, (grads[64:128] * gain_here)[None], grads[0:64][None]


def solution(mesh):
    in_specs = (
        P("dp", "section"),
        P("dp", "section"),
        P(),
        P("section", None),
        P("section", None, "dp"),
        P("section", None, "dp"),
    )
    out_specs = (
        P("section", "dp", None),
        P("section", "dp", None, None),
        P("section", None, "dp"),
        P("section", None, "dp"),
    )
    return jax.shard_map(body, mesh=mesh, in_specs=in_specs, out_specs=out_specs, check_vma=False)
```

```python
import jax
import jax.numpy as jnp
from jax import lax
from jax.experimental import pallas as pl
from jax.experimental.pallas import tpu as pltpu
from jax.sharding import PartitionSpec as P


EPS = 1e-05
SECT = 16
DP = 32
RANK = 64
D = 4096
F = 256
ROWS = 128
PAIR = 32
PIECE = 3712
BACK = 2432
GW = 1152
F32 = jnp.float32
BF = jnp.bfloat16
NT = (((1,), (1,)), ((), ()))
NN = (((1,), (0,)), ((), ()))
Y_GROUPS = [[2 * y + c for y in range(8)] for c in range(2)]
VMEM_LIMIT = 48 * 1024 * 1024


def dot(a, b, dims):
    return lax.dot_general(a, b, dims, preferred_element_type=F32)


def hi_lo(v):
    v = jnp.minimum(v, 3.0e38)
    hi = v.astype(BF).astype(F32)
    return hi, v - hi


def vmem(n):
    return [pl.BlockSpec(memory_space=pltpu.VMEM)] * n


SMEM = pl.BlockSpec(memory_space=pltpu.SMEM)


def gram_kernel(ints, w_ref, gkeep_ref, gsend_ref, wc_ref, uc_ref, pair_ref, gr_ref):
    p, quarter, core, source = ints[0], ints[1], ints[2], ints[3]
    taking = ints[4] > 0
    for s in range(SECT):
        for h in range(2):
            block = w_ref[4 * place_z(s) + 2 * (s % 2) + h, 0:128, :]
            lanes = slice(128 * h, 128 * h + 128)
            wc_ref[128 * s : 128 * s + 128, lanes] = block
            uc_ref[64 * s : 64 * s + 64, lanes] = block[64:128]
    for h in range(2):
        part = w_ref[source, 128 + 32 * h : 160 + 32 * h, :]
        pair_ref[:, 128 * h : 128 * h + 128] = jnp.where(taking, part, jnp.zeros_like(part))

    m = p // 2 + 1
    small_rows = wc_ref[pl.ds(pl.multiple_of(128 * p + 32 * quarter, 32), 32), :]
    big_rows = wc_ref[pl.ds(pl.multiple_of(128 * (15 - p) + 32 * quarter, 32), 32), :]
    small = dot(small_rows, uc_ref[0:512, :], NT)
    big = dot(big_rows, uc_ref[...], NT)
    st = [small[:, 128 * t : 128 * t + 128] for t in range(4)]
    tiles = [big[:, 128 * t : 128 * t + 128] for t in range(8)]
    tiles.append(st[3])
    for t in range(5, 9):
        for mm in range(1, 5):
            j = t - (9 - mm)
            if 0 <= j < 4:
                tiles[t] = jnp.where(m == mm, st[j], tiles[t])
    for t in range(9):
        gr_ref[:, 128 * t : 128 * t + 128] = tiles[t]
    for gref, part in ((gkeep_ref, core), (gsend_ref, 1 - core)):
        gref[...] = gr_ref[pl.ds(pl.multiple_of(16 * part, 16), 16), :].astype(BF)


def project_kernel(ints, x_ref, pair_ref, g_ref, wc_ref, uc_ref, o0, o1, o2, o3, res_ref, ex_ref):
    core, sec = ints[2], ints[5]
    x = x_ref[...]
    pair = pair_ref[...]
    res_ref[:, 0:2048] = dot(x, wc_ref[...], NT)
    res_ref[:, 2048:3072] = dot(g_ref[...], uc_ref[...], NT)
    extra = dot(pair, wc_ref[...], NT)
    for i in range(2):
        for k in range(4):
            for b in range(4):
                at = 512 * k + 128 * b
                ex_ref[pl.ds(128 * b + 4 * i + k, 16, stride=8), :] = extra[16 * i : 16 * i + 16, at : at + 128]
    for b in range(4):
        res_ref[:, 3072 + 128 * b : 3200 + 128 * b] = ex_ref[128 * b : 128 * b + 128, :]

    xf = x.astype(F32)
    pf = pair.astype(F32)
    own_hi, own_lo = hi_lo(jnp.sum(xf * xf, axis=1, keepdims=True))
    pair_hi, pair_lo = hi_lo(jnp.sum(pf * pf, axis=1, keepdims=True))
    ex_ref[0:ROWS, :] = jnp.zeros((ROWS, 128), F32)
    lane = lax.broadcasted_iota(jnp.int32, (PAIR, 128), 1) - 4 * sec
    pair_part = jnp.where(lane == 2, pair_hi, 0.0) + jnp.where(lane == 3, pair_lo, 0.0)
    for i in range(2):
        ex_ref[pl.ds(i, 16, stride=8), :] = pair_part[16 * i : 16 * i + 16]
    lane = lax.broadcasted_iota(jnp.int32, (ROWS, 128), 1) - 4 * sec
    own_part = jnp.where(lane == 0, own_hi, 0.0) + jnp.where(lane == 1, own_lo, 0.0)
    res_ref[:, 3584:3712] = ex_ref[0:ROWS, :] + own_part
    for k, ref in enumerate((o0, o1, o2, o3)):
        first = 64 * (core ^ (k % 2)) + 8 * (((sec >> 1) & 1) ^ (k // 2))
        for j in range(2):
            low = res_ref[pl.ds(pl.multiple_of(first + 32 * j, 8), 8), :]
            high = res_ref[pl.ds(pl.multiple_of(first + 32 * j + 16, 8), 8), :]
            ref[16 * j : 16 * j + 16, :] = jnp.concatenate([low, high], axis=0).astype(BF)


def slab_place(s):
    if s >= 8:
        return 15 - s, 0
    return s, 128 * (9 - (s // 2 + 1))


def recur_kernel(ints, sum_ref, mine_ref, other_ref, out_ref, slab_ref, pq_ref, h_ref, acc_ref, t_ref, pre_ref, ds_ref, ho_ref):
    core = ints[0]
    mine_row = pl.multiple_of(16 * core, 16)
    other_row = pl.multiple_of(16 * (1 - core), 16)
    for q in range(DP):
        base = 128 * (q // 4) + 32 * (q % 4)
        slab_ref[pl.ds(base + mine_row, 16), :] = mine_ref[q]
        slab_ref[pl.ds(base + other_row, 16), :] = other_ref[q]
    pq_ref[...] = jnp.zeros_like(pq_ref)
    pq_ref[0:8, :] = sum_ref[:, 0:3072]
    more = sum_ref[:, 3072:3584]
    for i in range(2):
        for k in range(4):
            pq_ref[8 + i : 9 + i, 512 * k : 512 * k + 512] = more[4 * i + k : 4 * i + k + 1]
    h_ref[...] = jnp.zeros_like(h_ref)
    acc_ref[...] = jnp.zeros_like(acc_ref)
    misc = sum_ref[:, 3584:3712]
    pair_lane = lax.broadcasted_iota(jnp.int32, (8, 128), 1) % 4 >= 2
    n_own = jnp.sum(jnp.where(pair_lane, 0.0, misc), axis=1, keepdims=True)
    n_pair = jnp.sum(jnp.where(pair_lane, misc, 0.0), axis=1, keepdims=True)
    n = jnp.concatenate([n_own, n_pair], axis=0)
    row = lax.broadcasted_iota(jnp.int32, (16, 1), 0)
    n = jnp.where(row < 10, n, 0.0)

    inverse = []
    zeros = jnp.zeros((16, RANK), BF)
    for s in range(SECT):
        place, off = slab_place(s)
        r0 = 128 * place
        depth = 128 * ((s + 1) // 2)
        tp = pq_ref[:, 128 * s : 128 * s + 64]
        tq = pq_ref[:, 128 * s + 64 : 128 * s + 128]
        if s:
            before = h_ref[:, 0:depth]
            tp = tp + dot(before, slab_ref[r0 : r0 + 64, off : off + depth], NT)
            tq = tq + dot(before, slab_ref[r0 + 64 : r0 + 128, off : off + depth], NT)
        inv = lax.rsqrt(jnp.maximum(n, 0.0) * (1.0 / D) + EPS)
        inverse.append(inv)
        pre = inv * tp
        sig = 0.5 + 0.5 * jnp.tanh(0.5 * pre)
        hf = pre * sig
        h = hf.astype(BF)
        pre_ref[:, 64 * s : 64 * s + 64] = pre
        ds_ref[:, 64 * s : 64 * s + 64] = sig * (1.0 + pre * (1.0 - sig))
        tile = slice(128 * (s // 2), 128 * (s // 2) + 128)
        own = jnp.concatenate([zeros, h] if s % 2 else [h, zeros], axis=1)
        h_ref[:, tile] = h_ref[:, tile] + own if s % 2 else own
        hd = dot(own, slab_ref[r0 + 64 : r0 + 128, off + tile.start : off + tile.stop], NT)
        n = n + jnp.sum(h.astype(F32) * (2.0 * tq + hd), axis=1, keepdims=True)
        t_ref[:, 64 * s : 64 * s + 64] = tq + hd

    lane16 = lax.broadcasted_iota(jnp.int32, (16, 128), 1)
    beta_sum = jnp.zeros((16, 1), F32)
    misc_out = jnp.zeros((16, 128), F32)
    for s in range(SECT - 1, -1, -1):
        place, off = slab_place(s)
        r0 = 128 * place
        cols = slice(64 * s, 64 * s + 64)
        inv = inverse[s]
        hf = h_ref[:, cols].astype(F32)
        dh = pq_ref[:, 2048 + 64 * s : 2048 + 64 * s + 64] + acc_ref[:, cols] - beta_sum * t_ref[:, cols]
        dp = (dh * ds_ref[:, cols]).astype(BF).astype(F32)
        beta = inv * inv * (jnp.sum(dp * pre_ref[:, cols], axis=1, keepdims=True) * (1.0 / D))
        z = (inv * dp).astype(BF)
        hb = (beta_sum * hf).astype(BF)
        depth = 128 * ((s + 1) // 2)
        for start in range(depth - 128, -1, -128):
            part = slice(start, start + 128)
            acc_ref[:, part] = (
                acc_ref[:, part]
                + dot(z, slab_ref[r0 : r0 + 64, off + start : off + start + 128], NN)
                - dot(hb, slab_ref[r0 + 64 : r0 + 128, off + start : off + start + 128], NN)
            )
        beta_sum = beta_sum + beta
        ho_ref[0:8, 1024 + 64 * s : 1024 + 64 * s + 64] = z[0:8].astype(F32)
        inv_hi, inv_lo = hi_lo(inv)
        misc_out = jnp.where(lane16 == s, beta, misc_out)
        misc_out = jnp.where(lane16 == 16 + s, inv_hi, misc_out)
        misc_out = jnp.where(lane16 == 32 + s, inv_lo, misc_out)
    h_all = h_ref[...].astype(F32)
    ho_ref[0:8, 0:1024] = h_all[0:8]
    for i in range(2):
        for k in range(4):
            ho_ref[4 * i + k : 4 * i + k + 1, 2048:2304] = h_all[8 + i : 9 + i, 256 * k : 256 * k + 256]
    extra_misc = pltpu.roll(misc_out[8:16], 32, 1)
    lane8 = lax.broadcasted_iota(jnp.int32, (8, 128), 1)
    row8 = lax.broadcasted_iota(jnp.int32, (8, 128), 0)
    keep = (lane8 >= 48) & (lane8 < 80) & (row8 < 2)
    ho_ref[0:8, 2304:2432] = jnp.where(keep, extra_misc, jnp.where(lane8 < 48, misc_out[0:8], 0.0))
    out_ref[...] = ho_ref[...].astype(BF)


def rebuild_kernel(ints, x_ref, pair_ref, mine_ref, other_ref, eh_ref, wc_ref, out_ref, back_ref):
    gather_rows(ints[3], mine_ref, other_ref, back_ref)
    own_at = pl.multiple_of(ints[0], 32)
    pair_at = pl.multiple_of(ints[1], 32)
    alive = ints[2] > 0
    x = x_ref[...].astype(F32)
    e = pair_ref[...].astype(F32)
    for s in range(SECT):
        out_ref[s, pl.ds(own_at, ROWS), :] = jnp.where(alive, x, 0.0).astype(BF)
        out_ref[s, pl.ds(pair_at, PAIR), :] = e.astype(BF)
        if s < SECT - 1:
            up = wc_ref[128 * s + 64 : 128 * s + 128, :]
            x = x + dot(back_ref[:, 64 * s : 64 * s + 64], up, NN)
            e = e + dot(eh_ref[:, 64 * s : 64 * s + 64], up, NN)


def gather_rows(core, mine_ref, other_ref, full_ref):
    full_ref[pl.ds(pl.multiple_of(64 * core, 64), 64), :] = mine_ref[...]
    full_ref[pl.ds(pl.multiple_of(64 * (1 - core), 64), 64), :] = other_ref[...]


def pick(values, index):
    out = values[0]
    for k in range(1, len(values)):
        out = jnp.where(index == k, values[k], out)
    return out


def grads_kernel(ints, x_ref, g_ref, mine_ref, other_ref, wc_ref, keep_ref, send_ref, back_ref, xs_ref, ht_ref, zt_ref):
    gather_rows(ints[0], mine_ref, other_ref, back_ref)
    along = ints[1]
    ht_ref[...] = back_ref[:, 0:1024].T
    zt_ref[...] = back_ref[:, 1024:2048].T
    x = x_ref[...].astype(F32)
    for s in range(SECT):
        xs_ref[s] = x.astype(BF)
        if s < SECT - 1:
            x = x + dot(back_ref[:, 64 * s : 64 * s + 64], wc_ref[128 * s + 64 : 128 * s + 128, :], NN)
    g = g_ref[...].astype(F32)
    betas = back_ref[:, 2304:2432].astype(F32)
    blocks = [None] * 4
    for s in range(SECT - 1, -1, -1):
        xs = xs_ref[s]
        up = dot(ht_ref[64 * s : 64 * s + 64, :], g.astype(BF), NN)
        down = dot(zt_ref[64 * s : 64 * s + 64, :], xs, NN)
        both = jnp.concatenate([up, down], axis=0).astype(BF)
        for h in range(2):
            blocks[2 * (s % 2) + h] = both[:, 128 * h : 128 * h + 128]
        if s % 2 == 0:
            for ref, flips in ((keep_ref, (0, 3)), (send_ref, (1, 2))):
                for k in range(2):
                    ref[k, place_z(s)] = pick(blocks, along ^ flips[k])
        if s:
            z = back_ref[:, 1024 + 64 * s : 1024 + 64 * s + 64]
            g = g + dot(z, wc_ref[128 * s : 128 * s + 64, :], NN) - betas[:, s : s + 1] * xs.astype(F32)


def join_kernel(in_ref, out_ref):
    for k in range(SECT):
        out_ref[0, 0, :, F * k : F * k + F] = in_ref[k]


def call(kernel, n_in, outs, scratch, flops, nbytes, with_ints=True):
    return pl.pallas_call(
        kernel,
        out_shape=outs,
        in_specs=([SMEM] if with_ints else []) + vmem(n_in),
        out_specs=jax.tree.map(lambda _: pl.BlockSpec(memory_space=pltpu.VMEM), outs),
        scratch_shapes=scratch,
        compiler_params=pltpu.CompilerParams(vmem_limit_bytes=VMEM_LIMIT),
        cost_estimate=pl.CostEstimate(flops=flops, bytes_accessed=nbytes, transcendentals=0),
    )


def shape(*dims, kind=BF):
    return jax.ShapeDtypeStruct(dims, kind)


def exchange(value, axis, groups=None):
    return lax.all_to_all(value, axis, 0, 0, tiled=True, axis_index_groups=groups)


def flip(value, bits):
    return lax.ppermute(value, "dp", [(i, i ^ bits) for i in range(DP)])


def scatter_sum(keep, send, me, later):
    value = keep.astype(F32) + flip(send, 1).astype(F32)
    value = value[0] + flip(value[1].astype(BF), 3).astype(F32)
    value, later = lax.optimization_barrier((value, later))
    blocks = value.astype(BF).reshape(2, 4, 128, 128)
    along = (me >> 2) & 3
    value = lax.dynamic_index_in_dim(value.reshape(2, 4, 128, 128), along, 1, keepdims=False)
    for k in (1, 2, 3):
        value = value + flip(lax.dynamic_index_in_dim(blocks, along ^ k, 1, keepdims=False), 4 * k).astype(F32)
    value = value.astype(BF)
    keep = lax.dynamic_index_in_dim(value, me >> 4, 0, keepdims=False)
    send = lax.dynamic_index_in_dim(value, 1 - (me >> 4), 0, keepdims=False)
    both = ("section", "dp")
    mine = lax.ppermute(keep, both, [(a, owner(a // DP, a % DP)) for a in range(SECT * DP)])
    theirs = lax.ppermute(send, both, [(a, owner(a // DP, a % DP ^ 16)) for a in range(SECT * DP)])
    return mine, theirs, later


def place_z(s):
    return (s // 2 - 2) % 8


def owner(sec, q):
    return (2 * ((q // 4 + 2) % 8) + q // 2 % 2) * DP + 2 * sec + q % 2


def body(x, g, worker, gain, narrow, widen):
    sec = lax.axis_index("section")
    me = lax.axis_index("dp")

    gain_here = lax.dynamic_slice(gain, (0, 128 * me), (1, 128))
    block = jnp.concatenate([(narrow[0].astype(F32) * gain_here).astype(BF), widen[0]], axis=0)
    block = lax.ppermute(block, ("section", "dp"), [(owner(a // DP, a % DP), a) for a in range(SECT * DP)])

    owners = jnp.arange(DP, dtype=jnp.int32)
    takers = worker[:, ::2]
    mine = lax.dynamic_index_in_dim(takers, me, 0, keepdims=False)
    alive = mine[0] == me
    comes = jnp.any((takers == me) & (owners != me)[:, None], axis=1)
    source = jnp.sum(jnp.where(comes, owners, 0))
    taking = jnp.any(comes)
    pair_first = taking & (source < me)
    goes = (mine[None, :] == owners[:, None]) & jnp.logical_not(alive)
    quads = jnp.concatenate([x[:, 0:128].reshape(4, PAIR, 128), x[:, 128:256].reshape(4, PAIR, 128)], axis=1)
    outgoing = jnp.zeros((DP, 2 * PAIR, 128), BF)
    for j in range(4):
        outgoing = jnp.where(goes[:, j][:, None, None], quads[j][None], outgoing)
    weights = jnp.concatenate([jnp.broadcast_to(block[None], (DP, 128, 128)), outgoing], axis=1)
    weights = exchange(weights, "dp")

    core = sec % 2
    ints = jnp.stack([me // 4, me % 4, core, source, taking.astype(jnp.int32), sec]).astype(jnp.int32)
    gkeep, gsend, wc, uc, pair = call(
        gram_kernel,
        1,
        (shape(16, GW), shape(16, GW), shape(2048, F), shape(1024, F), shape(PAIR, F)),
        [pltpu.VMEM((32, GW), F32)],
        10**8,
        3 * 10**6,
    )(ints, weights)
    swap = [(i, i ^ 1) for i in range(SECT)]
    share = (gkeep.astype(F32) + lax.ppermute(gsend, "section", swap).astype(F32)).astype(BF)
    parts = call(
        project_kernel,
        5,
        (shape(32, PIECE),) * 4,
        [pltpu.VMEM((ROWS, PIECE), F32), pltpu.VMEM((4 * ROWS, 128), F32)],
        3 * 10**8,
        3 * 10**6,
    )(ints, x, pair, g, wc, uc)
    share = exchange(jnp.broadcast_to(share[None], (8, 16, GW)), "section", Y_GROUPS)
    share = jnp.sum(share.astype(F32), axis=0).astype(BF)
    half = exchange(jnp.broadcast_to(share[None], (DP, 16, GW)), "dp")

    rows = parts[0].astype(F32)
    for k in range(1, 4):
        rows = rows + lax.ppermute(parts[k], "section", [(i, i ^ k) for i in range(SECT)]).astype(F32)
    rows = rows.astype(BF).reshape(4, 8, PIECE)
    here = sec // 4
    total = lax.dynamic_index_in_dim(rows, here, 0, keepdims=False).astype(F32)
    for k in range(1, 4):
        send = lax.dynamic_index_in_dim(rows, here ^ k, 0, keepdims=False)
        total = total + lax.ppermute(send, "section", [(i, i ^ (4 * k)) for i in range(SECT)]).astype(F32)
    half, total = lax.optimization_barrier((half, total))
    other = lax.ppermute(half, "section", swap)

    back = call(
        recur_kernel,
        3,
        shape(8, BACK),
        [
            pltpu.VMEM((1024, GW), BF),
            pltpu.VMEM((16, 3072), F32),
            pltpu.VMEM((16, 1024), BF),
            pltpu.VMEM((16, 1024), F32),
            pltpu.VMEM((16, 1024), F32),
            pltpu.VMEM((16, 1024), F32),
            pltpu.VMEM((16, 1024), F32),
            pltpu.VMEM((8, BACK), F32),
        ],
        2 * 10**8,
        3 * 10**6,
    )(core.reshape(1).astype(jnp.int32), total, half, other)
    back = exchange(jnp.broadcast_to(back[None], (8, 8, BACK)), "section", Y_GROUPS).reshape(64, BACK)
    back_other = lax.ppermute(back, "section", swap)

    blocks = call(
        grads_kernel,
        5,
        (shape(2, 8, 128, 128),) * 2,
        [
            pltpu.VMEM((ROWS, BACK), BF),
            pltpu.VMEM((SECT, ROWS, F), BF),
            pltpu.VMEM((1024, ROWS), BF),
            pltpu.VMEM((1024, ROWS), BF),
        ],
        3 * 10**8,
        3 * 10**6,
    )(jnp.stack([core, me % 4]).astype(jnp.int32), x, g, back, back_other, wc)

    small, small_other = back[:, 2048:2432], back_other[:, 2048:2432]
    small = jnp.where(
        core == 0, jnp.concatenate([small, small_other], axis=0), jnp.concatenate([small_other, small], axis=0)
    ).reshape(SECT, 8, 384)
    extra_h = small[:, :, 0:256].reshape(SECT, 2, 4, 256).transpose(1, 0, 2, 3).reshape(PAIR, 1024)
    own_at = jnp.where(pair_first, PAIR, 0)
    pair_at = jnp.where(pair_first, 0, ROWS)
    rows_out = call(
        rebuild_kernel,
        6,
        shape(SECT, ROWS + PAIR, F),
        [pltpu.VMEM((ROWS, BACK), BF)],
        2 * 10**8,
        3 * 10**6,
    )(jnp.stack([own_at, pair_at, alive.astype(jnp.int32), core]).astype(jnp.int32), x, pair, back, back_other, extra_h, wc)
    saved = exchange(rows_out, "section")
    misc = small[:, :, 256:384]
    mine_sum, other_sum, misc = scatter_sum(*blocks, me, misc)
    saved = call(join_kernel, 1, shape(1, 1, ROWS + PAIR, D), [], 0, 3 * 10**6, False)(saved)

    saved, mine_sum, other_sum = lax.optimization_barrier((saved, mine_sum, other_sum))
    grads = mine_sum.astype(F32) + other_sum.astype(F32)

    misc = misc.astype(F32)
    own_inv = misc[:, :, 16:32] + misc[:, :, 32:48]
    pair_inv = misc[:, 0:2, 48:64] + misc[:, 0:2, 64:80]
    own_inv = lax.dynamic_index_in_dim(own_inv, sec, 2, keepdims=False).reshape(ROWS)
    pair_inv = lax.dynamic_index_in_dim(pair_inv, sec, 2, keepdims=False).T.reshape(PAIR)
    own_inv = jnp.where(alive, own_inv, 0.0)
    pair_inv = jnp.where(taking, pair_inv, 0.0)
    rstd = jnp.where(
        pair_first, jnp.concatenate([pair_inv, own_inv]), jnp.concatenate([own_inv, pair_inv])
    ).reshape(1, 1, ROWS + PAIR)
    return rstd, saved, (grads[64:128] * gain_here)[None], grads[0:64][None]


def solution(mesh):
    in_specs = (
        P("dp", "section"),
        P("dp", "section"),
        P(),
        P("section", None),
        P("section", None, "dp"),
        P("section", None, "dp"),
    )
    out_specs = (
        P("section", "dp", None),
        P("section", "dp", None, None),
        P("section", None, "dp"),
        P("section", None, "dp"),
    )
    return jax.shard_map(body, mesh=mesh, in_specs=in_specs, out_specs=out_specs, check_vma=False)
```

```python
import jax
import jax.numpy as jnp
from jax import lax
from jax.experimental import pallas as pl
from jax.experimental.pallas import tpu as pltpu
from jax.sharding import PartitionSpec as P


EPS = 1e-05
SECT = 16
DP = 32
RANK = 64
D = 4096
F = 256
ROWS = 128
PAIR = 32
PIECE = 3712
BACK = 2432
GW = 1152
F32 = jnp.float32
BF = jnp.bfloat16
NT = (((1,), (1,)), ((), ()))
NN = (((1,), (0,)), ((), ()))
Y_GROUPS = [[2 * (2 * k + low) + c for low in range(2) for k in range(4)] for c in range(2)]
VMEM_LIMIT = 48 * 1024 * 1024


def dot(a, b, dims):
    return lax.dot_general(a, b, dims, preferred_element_type=F32)


def hi_lo(v):
    v = jnp.minimum(v, 3.0e38)
    hi = v.astype(BF).astype(F32)
    return hi, v - hi


def vmem(n):
    return [pl.BlockSpec(memory_space=pltpu.VMEM)] * n


SMEM = pl.BlockSpec(memory_space=pltpu.SMEM)


def gram_kernel(ints, w_ref, gkeep_ref, gsend_ref, wc_ref, uc_ref, pair_ref, gr_ref):
    p, quarter, core, source = ints[0], ints[1], ints[2], ints[3]
    taking = ints[4] > 0
    for s in range(SECT):
        for h in range(2):
            block = w_ref[4 * place_z(s) + 2 * (s % 2) + h, 0:128, :]
            lanes = slice(128 * h, 128 * h + 128)
            wc_ref[128 * s : 128 * s + 128, lanes] = block
            uc_ref[64 * s : 64 * s + 64, lanes] = block[64:128]
    for h in range(2):
        part = w_ref[source, 128 + 32 * h : 160 + 32 * h, :]
        pair_ref[:, 128 * h : 128 * h + 128] = jnp.where(taking, part, jnp.zeros_like(part))

    m = p // 2 + 1
    small_rows = wc_ref[pl.ds(pl.multiple_of(128 * p + 32 * quarter, 32), 32), :]
    big_rows = wc_ref[pl.ds(pl.multiple_of(128 * (15 - p) + 32 * quarter, 32), 32), :]
    small = dot(small_rows, uc_ref[0:512, :], NT)
    big = dot(big_rows, uc_ref[...], NT)
    st = [small[:, 128 * t : 128 * t + 128] for t in range(4)]
    tiles = [big[:, 128 * t : 128 * t + 128] for t in range(8)]
    tiles.append(st[3])
    for t in range(5, 9):
        for mm in range(1, 5):
            j = t - (9 - mm)
            if 0 <= j < 4:
                tiles[t] = jnp.where(m == mm, st[j], tiles[t])
    for t in range(9):
        gr_ref[:, 128 * t : 128 * t + 128] = tiles[t]
    for gref, part in ((gkeep_ref, core), (gsend_ref, 1 - core)):
        gref[...] = gr_ref[pl.ds(pl.multiple_of(16 * part, 16), 16), :].astype(BF)


def project_kernel(ints, x_ref, pair_ref, g_ref, wc_ref, uc_ref, o0, o1, o2, o3, res_ref, ex_ref):
    core, sec = ints[2], ints[5]
    x = x_ref[...]
    pair = pair_ref[...]
    res_ref[:, 0:2048] = dot(x, wc_ref[...], NT)
    res_ref[:, 2048:3072] = dot(g_ref[...], uc_ref[...], NT)
    extra = dot(pair, wc_ref[...], NT)
    for i in range(2):
        for k in range(4):
            for b in range(4):
                at = 512 * k + 128 * b
                ex_ref[pl.ds(128 * b + 4 * i + k, 16, stride=8), :] = extra[16 * i : 16 * i + 16, at : at + 128]
    for b in range(4):
        res_ref[:, 3072 + 128 * b : 3200 + 128 * b] = ex_ref[128 * b : 128 * b + 128, :]

    xf = x.astype(F32)
    pf = pair.astype(F32)
    own_hi, own_lo = hi_lo(jnp.sum(xf * xf, axis=1, keepdims=True))
    pair_hi, pair_lo = hi_lo(jnp.sum(pf * pf, axis=1, keepdims=True))
    ex_ref[0:ROWS, :] = jnp.zeros((ROWS, 128), F32)
    lane = lax.broadcasted_iota(jnp.int32, (PAIR, 128), 1) - 4 * sec
    pair_part = jnp.where(lane == 2, pair_hi, 0.0) + jnp.where(lane == 3, pair_lo, 0.0)
    for i in range(2):
        ex_ref[pl.ds(i, 16, stride=8), :] = pair_part[16 * i : 16 * i + 16]
    lane = lax.broadcasted_iota(jnp.int32, (ROWS, 128), 1) - 4 * sec
    own_part = jnp.where(lane == 0, own_hi, 0.0) + jnp.where(lane == 1, own_lo, 0.0)
    res_ref[:, 3584:3712] = ex_ref[0:ROWS, :] + own_part
    for k, ref in enumerate((o0, o1, o2, o3)):
        first = 64 * (core ^ (k % 2)) + 32 * (((sec >> 1) & 1) ^ (k // 2))
        ref[...] = res_ref[pl.ds(pl.multiple_of(first, 32), 32), :].astype(BF)


def slab_place(s):
    if s >= 8:
        return 15 - s, 0
    return s, 128 * (9 - (s // 2 + 1))


def recur_kernel(ints, sum_ref, mine_ref, other_ref, out_ref, slab_ref, pq_ref, h_ref, acc_ref, t_ref, pre_ref, ds_ref, ho_ref):
    core = ints[0]
    mine_row = pl.multiple_of(16 * core, 16)
    other_row = pl.multiple_of(16 * (1 - core), 16)
    for q in range(DP):
        base = 128 * (q // 4) + 32 * (q % 4)
        slab_ref[pl.ds(base + mine_row, 16), :] = mine_ref[q]
        slab_ref[pl.ds(base + other_row, 16), :] = other_ref[q]
    pq_ref[...] = jnp.zeros_like(pq_ref)
    pq_ref[0:8, :] = sum_ref[:, 0:3072]
    more = sum_ref[:, 3072:3584]
    for i in range(2):
        for k in range(4):
            pq_ref[8 + i : 9 + i, 512 * k : 512 * k + 512] = more[4 * i + k : 4 * i + k + 1]
    h_ref[...] = jnp.zeros_like(h_ref)
    acc_ref[...] = jnp.zeros_like(acc_ref)
    misc = sum_ref[:, 3584:3712]
    pair_lane = lax.broadcasted_iota(jnp.int32, (8, 128), 1) % 4 >= 2
    n_own = jnp.sum(jnp.where(pair_lane, 0.0, misc), axis=1, keepdims=True)
    n_pair = jnp.sum(jnp.where(pair_lane, misc, 0.0), axis=1, keepdims=True)
    n = jnp.concatenate([n_own, n_pair], axis=0)
    row = lax.broadcasted_iota(jnp.int32, (16, 1), 0)
    n = jnp.where(row < 10, n, 0.0)

    inverse = []
    zeros = jnp.zeros((16, RANK), BF)
    for s in range(SECT):
        place, off = slab_place(s)
        r0 = 128 * place
        depth = 128 * ((s + 1) // 2)
        tp = pq_ref[:, 128 * s : 128 * s + 64]
        tq = pq_ref[:, 128 * s + 64 : 128 * s + 128]
        if s:
            before = h_ref[:, 0:depth]
            tp = tp + dot(before, slab_ref[r0 : r0 + 64, off : off + depth], NT)
            tq = tq + dot(before, slab_ref[r0 + 64 : r0 + 128, off : off + depth], NT)
        inv = lax.rsqrt(jnp.maximum(n, 0.0) * (1.0 / D) + EPS)
        inverse.append(inv)
        pre = inv * tp
        sig = 0.5 + 0.5 * jnp.tanh(0.5 * pre)
        hf = pre * sig
        h = hf.astype(BF)
        pre_ref[:, 64 * s : 64 * s + 64] = pre
        ds_ref[:, 64 * s : 64 * s + 64] = sig * (1.0 + pre * (1.0 - sig))
        tile = slice(128 * (s // 2), 128 * (s // 2) + 128)
        own = jnp.concatenate([zeros, h] if s % 2 else [h, zeros], axis=1)
        h_ref[:, tile] = h_ref[:, tile] + own if s % 2 else own
        hd = dot(own, slab_ref[r0 + 64 : r0 + 128, off + tile.start : off + tile.stop], NT)
        n = n + jnp.sum(h.astype(F32) * (2.0 * tq + hd), axis=1, keepdims=True)
        t_ref[:, 64 * s : 64 * s + 64] = tq + hd

    lane16 = lax.broadcasted_iota(jnp.int32, (16, 128), 1)
    beta_sum = jnp.zeros((16, 1), F32)
    misc_out = jnp.zeros((16, 128), F32)
    for s in range(SECT - 1, -1, -1):
        place, off = slab_place(s)
        r0 = 128 * place
        cols = slice(64 * s, 64 * s + 64)
        inv = inverse[s]
        hf = h_ref[:, cols].astype(F32)
        dh = pq_ref[:, 2048 + 64 * s : 2048 + 64 * s + 64] + acc_ref[:, cols] - beta_sum * t_ref[:, cols]
        dp = (dh * ds_ref[:, cols]).astype(BF).astype(F32)
        beta = inv * inv * (jnp.sum(dp * pre_ref[:, cols], axis=1, keepdims=True) * (1.0 / D))
        z = (inv * dp).astype(BF)
        hb = (beta_sum * hf).astype(BF)
        depth = 128 * ((s + 1) // 2)
        for start in range(depth - 128, -1, -128):
            part = slice(start, start + 128)
            acc_ref[:, part] = (
                acc_ref[:, part]
                + dot(z, slab_ref[r0 : r0 + 64, off + start : off + start + 128], NN)
                - dot(hb, slab_ref[r0 + 64 : r0 + 128, off + start : off + start + 128], NN)
            )
        beta_sum = beta_sum + beta
        ho_ref[0:8, 1024 + 64 * s : 1024 + 64 * s + 64] = z[0:8].astype(F32)
        inv_hi, inv_lo = hi_lo(inv)
        misc_out = jnp.where(lane16 == s, beta, misc_out)
        misc_out = jnp.where(lane16 == 16 + s, inv_hi, misc_out)
        misc_out = jnp.where(lane16 == 32 + s, inv_lo, misc_out)
    h_all = h_ref[...].astype(F32)
    ho_ref[0:8, 0:1024] = h_all[0:8]
    for i in range(2):
        for k in range(4):
            ho_ref[4 * i + k : 4 * i + k + 1, 2048:2304] = h_all[8 + i : 9 + i, 256 * k : 256 * k + 256]
    extra_misc = pltpu.roll(misc_out[8:16], 32, 1)
    lane8 = lax.broadcasted_iota(jnp.int32, (8, 128), 1)
    row8 = lax.broadcasted_iota(jnp.int32, (8, 128), 0)
    keep = (lane8 >= 48) & (lane8 < 80) & (row8 < 2)
    ho_ref[0:8, 2304:2432] = jnp.where(keep, extra_misc, jnp.where(lane8 < 48, misc_out[0:8], 0.0))
    out_ref[...] = ho_ref[...].astype(BF)


def rebuild_kernel(ints, x_ref, pair_ref, mine_ref, other_ref, eh_ref, wc_ref, out_ref, back_ref):
    gather_rows(ints[3], mine_ref, other_ref, back_ref)
    own_at = pl.multiple_of(ints[0], 32)
    pair_at = pl.multiple_of(ints[1], 32)
    alive = ints[2] > 0
    x = x_ref[...].astype(F32)
    e = pair_ref[...].astype(F32)
    for s in range(SECT):
        out_ref[s, pl.ds(own_at, ROWS), :] = jnp.where(alive, x, 0.0).astype(BF)
        out_ref[s, pl.ds(pair_at, PAIR), :] = e.astype(BF)
        if s < SECT - 1:
            up = wc_ref[128 * s + 64 : 128 * s + 128, :]
            x = x + dot(back_ref[:, 64 * s : 64 * s + 64], up, NN)
            e = e + dot(eh_ref[:, 64 * s : 64 * s + 64], up, NN)


def gather_rows(core, mine_ref, other_ref, full_ref):
    full_ref[pl.ds(pl.multiple_of(64 * core, 64), 64), :] = mine_ref[...]
    full_ref[pl.ds(pl.multiple_of(64 * (1 - core), 64), 64), :] = other_ref[...]


def pick(values, index):
    out = values[0]
    for k in range(1, len(values)):
        out = jnp.where(index == k, values[k], out)
    return out


def grads_kernel(ints, x_ref, g_ref, mine_ref, other_ref, wc_ref, keep_ref, send_ref, back_ref, xs_ref, ht_ref, zt_ref):
    gather_rows(ints[0], mine_ref, other_ref, back_ref)
    along = ints[1]
    ht_ref[...] = back_ref[:, 0:1024].T
    zt_ref[...] = back_ref[:, 1024:2048].T
    x = x_ref[...].astype(F32)
    for s in range(SECT):
        xs_ref[s] = x.astype(BF)
        if s < SECT - 1:
            x = x + dot(back_ref[:, 64 * s : 64 * s + 64], wc_ref[128 * s + 64 : 128 * s + 128, :], NN)
    g = g_ref[...].astype(F32)
    betas = back_ref[:, 2304:2432].astype(F32)
    blocks = [None] * 4
    for s in range(SECT - 1, -1, -1):
        xs = xs_ref[s]
        up = dot(ht_ref[64 * s : 64 * s + 64, :], g.astype(BF), NN)
        down = dot(zt_ref[64 * s : 64 * s + 64, :], xs, NN)
        both = jnp.concatenate([up, down], axis=0).astype(BF)
        for h in range(2):
            blocks[2 * (s % 2) + h] = both[:, 128 * h : 128 * h + 128]
        if s % 2 == 0:
            for ref, flips in ((keep_ref, (0, 3)), (send_ref, (1, 2))):
                for k in range(2):
                    ref[k, place_z(s)] = pick(blocks, along ^ flips[k])
        if s:
            z = back_ref[:, 1024 + 64 * s : 1024 + 64 * s + 64]
            g = g + dot(z, wc_ref[128 * s : 128 * s + 64, :], NN) - betas[:, s : s + 1] * xs.astype(F32)


def join_kernel(in_ref, out_ref):
    for k in range(SECT):
        out_ref[0, 0, :, F * k : F * k + F] = in_ref[k]


def call(kernel, n_in, outs, scratch, flops, nbytes, with_ints=True):
    return pl.pallas_call(
        kernel,
        out_shape=outs,
        in_specs=([SMEM] if with_ints else []) + vmem(n_in),
        out_specs=jax.tree.map(lambda _: pl.BlockSpec(memory_space=pltpu.VMEM), outs),
        scratch_shapes=scratch,
        compiler_params=pltpu.CompilerParams(vmem_limit_bytes=VMEM_LIMIT),
        cost_estimate=pl.CostEstimate(flops=flops, bytes_accessed=nbytes, transcendentals=0),
    )


def shape(*dims, kind=BF):
    return jax.ShapeDtypeStruct(dims, kind)


def exchange(value, axis, groups=None):
    return lax.all_to_all(value, axis, 0, 0, tiled=True, axis_index_groups=groups)


def flip(value, bits):
    return lax.ppermute(value, "dp", [(i, i ^ bits) for i in range(DP)])


def scatter_sum(keep, send, me, later):
    first = flip(send, 1)
    low = (me >> 2) & 1
    arrived = 0.0
    for e, b in ((1, 0), (0, 1), (1, 1)):
        part = keep[e].astype(F32) + first[e].astype(F32)
        part = lax.dynamic_index_in_dim(part.astype(BF).reshape(4, 2, 128, 128), low ^ b, 1, keepdims=False)
        arrived = arrived + flip(part, 3 * e | 4 * b).astype(F32)
    own = (keep[0].astype(F32) + first[0].astype(F32)).reshape(4, 2, 128, 128)
    value = lax.dynamic_index_in_dim(own, low, 1, keepdims=False) + arrived
    value, later = lax.optimization_barrier((value, later))
    middle = (me >> 3) & 1
    value = value.reshape(2, 2, 128, 128)
    send = lax.dynamic_index_in_dim(value, 1 - middle, 1, keepdims=False).astype(BF)
    value = (lax.dynamic_index_in_dim(value, middle, 1, keepdims=False) + flip(send, 8).astype(F32)).astype(BF)
    keep = lax.dynamic_index_in_dim(value, me >> 4, 0, keepdims=False)
    send = lax.dynamic_index_in_dim(value, 1 - (me >> 4), 0, keepdims=False)
    both = ("section", "dp")
    mine = lax.ppermute(keep, both, [(a, owner(a // DP, a % DP)) for a in range(SECT * DP)])
    theirs = lax.ppermute(send, both, [(a, owner(a // DP, a % DP ^ 16)) for a in range(SECT * DP)])
    return mine, theirs, later


def place_z(s):
    return (s // 2 - 2) % 8


def owner(sec, q):
    return (2 * ((q // 4 + 2) % 8) + q // 2 % 2) * DP + 2 * sec + q % 2


def body(x, g, worker, gain, narrow, widen):
    sec = lax.axis_index("section")
    me = lax.axis_index("dp")

    gain_here = lax.dynamic_slice(gain, (0, 128 * me), (1, 128))
    block = jnp.concatenate([(narrow[0].astype(F32) * gain_here).astype(BF), widen[0]], axis=0)
    block = lax.ppermute(block, ("section", "dp"), [(owner(a // DP, a % DP), a) for a in range(SECT * DP)])

    owners = jnp.arange(DP, dtype=jnp.int32)
    takers = worker[:, ::2]
    mine = lax.dynamic_index_in_dim(takers, me, 0, keepdims=False)
    alive = mine[0] == me
    comes = jnp.any((takers == me) & (owners != me)[:, None], axis=1)
    source = jnp.sum(jnp.where(comes, owners, 0))
    taking = jnp.any(comes)
    pair_first = taking & (source < me)
    goes = (mine[None, :] == owners[:, None]) & jnp.logical_not(alive)
    quads = jnp.concatenate([x[:, 0:128].reshape(4, PAIR, 128), x[:, 128:256].reshape(4, PAIR, 128)], axis=1)
    outgoing = jnp.zeros((DP, 2 * PAIR, 128), BF)
    for j in range(4):
        outgoing = jnp.where(goes[:, j][:, None, None], quads[j][None], outgoing)
    weights = jnp.concatenate([jnp.broadcast_to(block[None], (DP, 128, 128)), outgoing], axis=1)
    weights = exchange(weights, "dp")

    core = sec % 2
    ints = jnp.stack([me // 4, me % 4, core, source, taking.astype(jnp.int32), sec]).astype(jnp.int32)
    gkeep, gsend, wc, uc, pair = call(
        gram_kernel,
        1,
        (shape(16, GW), shape(16, GW), shape(2048, F), shape(1024, F), shape(PAIR, F)),
        [pltpu.VMEM((32, GW), F32)],
        10**8,
        3 * 10**6,
    )(ints, weights)
    swap = [(i, i ^ 1) for i in range(SECT)]
    share = (gkeep.astype(F32) + lax.ppermute(gsend, "section", swap).astype(F32)).astype(BF)
    parts = call(
        project_kernel,
        5,
        (shape(32, PIECE),) * 4,
        [pltpu.VMEM((ROWS, PIECE), F32), pltpu.VMEM((4 * ROWS, 128), F32)],
        3 * 10**8,
        3 * 10**6,
    )(ints, x, pair, g, wc, uc)
    share = exchange(jnp.broadcast_to(share[None], (8, 16, GW)), "section", Y_GROUPS)
    share = jnp.sum(share.astype(F32), axis=0).astype(BF)
    half = exchange(jnp.broadcast_to(share[None], (DP, 16, GW)), "dp")

    rows = parts[0].astype(F32)
    for k in range(1, 4):
        rows = rows + lax.ppermute(parts[k], "section", [(i, i ^ k) for i in range(SECT)]).astype(F32)
    rows = rows.astype(BF).reshape(4, 8, PIECE)
    here = sec // 4
    total = lax.dynamic_index_in_dim(rows, here, 0, keepdims=False).astype(F32)
    for k in range(1, 4):
        send = lax.dynamic_index_in_dim(rows, here ^ k, 0, keepdims=False)
        total = total + lax.ppermute(send, "section", [(i, i ^ (4 * k)) for i in range(SECT)]).astype(F32)
    half, total = lax.optimization_barrier((half, total))
    other = lax.ppermute(half, "section", swap)

    back = call(
        recur_kernel,
        3,
        shape(8, BACK),
        [
            pltpu.VMEM((1024, GW), BF),
            pltpu.VMEM((16, 3072), F32),
            pltpu.VMEM((16, 1024), BF),
            pltpu.VMEM((16, 1024), F32),
            pltpu.VMEM((16, 1024), F32),
            pltpu.VMEM((16, 1024), F32),
            pltpu.VMEM((16, 1024), F32),
            pltpu.VMEM((8, BACK), F32),
        ],
        2 * 10**8,
        3 * 10**6,
    )(core.reshape(1).astype(jnp.int32), total, half, other)
    back = exchange(jnp.broadcast_to(back[None], (8, 8, BACK)), "section", Y_GROUPS).reshape(64, BACK)
    back_other = lax.ppermute(back, "section", swap)

    blocks = call(
        grads_kernel,
        5,
        (shape(2, 8, 128, 128),) * 2,
        [
            pltpu.VMEM((ROWS, BACK), BF),
            pltpu.VMEM((SECT, ROWS, F), BF),
            pltpu.VMEM((1024, ROWS), BF),
            pltpu.VMEM((1024, ROWS), BF),
        ],
        3 * 10**8,
        3 * 10**6,
    )(jnp.stack([core, me % 4]).astype(jnp.int32), x, g, back, back_other, wc)

    small, small_other = back[:, 2048:2432], back_other[:, 2048:2432]
    small = jnp.where(
        core == 0, jnp.concatenate([small, small_other], axis=0), jnp.concatenate([small_other, small], axis=0)
    ).reshape(SECT, 8, 384)
    extra_h = small[:, :, 0:256].reshape(SECT, 2, 4, 256).transpose(1, 0, 2, 3).reshape(PAIR, 1024)
    own_at = jnp.where(pair_first, PAIR, 0)
    pair_at = jnp.where(pair_first, 0, ROWS)
    rows_out = call(
        rebuild_kernel,
        6,
        shape(SECT, ROWS + PAIR, F),
        [pltpu.VMEM((ROWS, BACK), BF)],
        2 * 10**8,
        3 * 10**6,
    )(jnp.stack([own_at, pair_at, alive.astype(jnp.int32), core]).astype(jnp.int32), x, pair, back, back_other, extra_h, wc)
    saved = exchange(rows_out, "section")
    misc = small[:, :, 256:384]
    mine_sum, other_sum, misc = scatter_sum(*blocks, me, misc)
    saved = call(join_kernel, 1, shape(1, 1, ROWS + PAIR, D), [], 0, 3 * 10**6, False)(saved)

    saved, mine_sum, other_sum = lax.optimization_barrier((saved, mine_sum, other_sum))
    grads = mine_sum.astype(F32) + other_sum.astype(F32)

    misc = misc.astype(F32)
    own_inv = misc[:, :, 16:32] + misc[:, :, 32:48]
    pair_inv = misc[:, 0:2, 48:64] + misc[:, 0:2, 64:80]
    own_inv = lax.dynamic_index_in_dim(own_inv, sec, 2, keepdims=False).reshape(ROWS)
    pair_inv = lax.dynamic_index_in_dim(pair_inv, sec, 2, keepdims=False).T.reshape(PAIR)
    own_inv = jnp.where(alive, own_inv, 0.0)
    pair_inv = jnp.where(taking, pair_inv, 0.0)
    rstd = jnp.where(
        pair_first, jnp.concatenate([pair_inv, own_inv]), jnp.concatenate([own_inv, pair_inv])
    ).reshape(1, 1, ROWS + PAIR)
    return rstd, saved, (grads[64:128] * gain_here)[None], grads[0:64][None]


def solution(mesh):
    in_specs = (
        P("dp", "section"),
        P("dp", "section"),
        P(),
        P("section", None),
        P("section", None, "dp"),
        P("section", None, "dp"),
    )
    out_specs = (
        P("section", "dp", None),
        P("section", "dp", None, None),
        P("section", None, "dp"),
        P("section", None, "dp"),
    )
    return jax.shard_map(body, mesh=mesh, in_specs=in_specs, out_specs=out_specs, check_vma=False)
```

```python
import jax
import jax.numpy as jnp
from jax import lax
from jax.experimental import pallas as pl
from jax.experimental.pallas import tpu as pltpu
from jax.sharding import PartitionSpec as P


EPS = 1e-05
SECT = 16
DP = 32
RANK = 64
D = 4096
F = 256
ROWS = 128
PAIR = 32
PIECE = 3712
BACK = 2432
GW = 1152
F32 = jnp.float32
BF = jnp.bfloat16
NT = (((1,), (1,)), ((), ()))
NN = (((1,), (0,)), ((), ()))
Y_GROUPS = [[2 * (2 * k + low) + c for low in range(2) for k in range(4)] for c in range(2)]
VMEM_LIMIT = 48 * 1024 * 1024


def dot(a, b, dims):
    return lax.dot_general(a, b, dims, preferred_element_type=F32)


def hi_lo(v):
    v = jnp.minimum(v, 3.0e38)
    hi = v.astype(BF).astype(F32)
    return hi, v - hi


def vmem(n):
    return [pl.BlockSpec(memory_space=pltpu.VMEM)] * n


SMEM = pl.BlockSpec(memory_space=pltpu.SMEM)


def gram_kernel(ints, w_ref, gkeep_ref, gsend_ref, wc_ref, uc_ref, pair_ref, gr_ref):
    p, quarter, core, source = ints[0], ints[1], ints[2], ints[3]
    taking = ints[4] > 0
    for s in range(SECT):
        for h in range(2):
            block = w_ref[4 * place_z(s) + 2 * (s % 2) + h, 0:128, :]
            lanes = slice(128 * h, 128 * h + 128)
            wc_ref[128 * s : 128 * s + 128, lanes] = block
            uc_ref[64 * s : 64 * s + 64, lanes] = block[64:128]
    for h in range(2):
        part = w_ref[source, 128 + 32 * h : 160 + 32 * h, :]
        pair_ref[:, 128 * h : 128 * h + 128] = jnp.where(taking, part, jnp.zeros_like(part))

    m = p // 2 + 1
    small_rows = wc_ref[pl.ds(pl.multiple_of(128 * p + 32 * quarter, 32), 32), :]
    big_rows = wc_ref[pl.ds(pl.multiple_of(128 * (15 - p) + 32 * quarter, 32), 32), :]
    small = dot(small_rows, uc_ref[0:512, :], NT)
    big = dot(big_rows, uc_ref[...], NT)
    st = [small[:, 128 * t : 128 * t + 128] for t in range(4)]
    tiles = [big[:, 128 * t : 128 * t + 128] for t in range(8)]
    tiles.append(st[3])
    for t in range(5, 9):
        for mm in range(1, 5):
            j = t - (9 - mm)
            if 0 <= j < 4:
                tiles[t] = jnp.where(m == mm, st[j], tiles[t])
    for t in range(9):
        gr_ref[:, 128 * t : 128 * t + 128] = tiles[t]
    for gref, part in ((gkeep_ref, core), (gsend_ref, 1 - core)):
        gref[...] = gr_ref[pl.ds(pl.multiple_of(16 * part, 16), 16), :].astype(BF)


def project_kernel(ints, x_ref, pair_ref, g_ref, wc_ref, uc_ref, o0, o1, o2, o3, res_ref, ex_ref):
    core, sec = ints[2], ints[5]
    x = x_ref[...]
    pair = pair_ref[...]
    res_ref[:, 0:2048] = dot(x, wc_ref[...], NT)
    res_ref[:, 2048:3072] = dot(g_ref[...], uc_ref[...], NT)
    extra = dot(pair, wc_ref[...], NT)
    for i in range(2):
        for k in range(4):
            for b in range(4):
                at = 512 * k + 128 * b
                ex_ref[pl.ds(128 * b + 4 * i + k, 16, stride=8), :] = extra[16 * i : 16 * i + 16, at : at + 128]
    for b in range(4):
        res_ref[:, 3072 + 128 * b : 3200 + 128 * b] = ex_ref[128 * b : 128 * b + 128, :]

    xf = x.astype(F32)
    pf = pair.astype(F32)
    own_hi, own_lo = hi_lo(jnp.sum(xf * xf, axis=1, keepdims=True))
    pair_hi, pair_lo = hi_lo(jnp.sum(pf * pf, axis=1, keepdims=True))
    ex_ref[0:ROWS, :] = jnp.zeros((ROWS, 128), F32)
    lane = lax.broadcasted_iota(jnp.int32, (PAIR, 128), 1) - 4 * sec
    pair_part = jnp.where(lane == 2, pair_hi, 0.0) + jnp.where(lane == 3, pair_lo, 0.0)
    for i in range(2):
        ex_ref[pl.ds(i, 16, stride=8), :] = pair_part[16 * i : 16 * i + 16]
    lane = lax.broadcasted_iota(jnp.int32, (ROWS, 128), 1) - 4 * sec
    own_part = jnp.where(lane == 0, own_hi, 0.0) + jnp.where(lane == 1, own_lo, 0.0)
    res_ref[:, 3584:3712] = ex_ref[0:ROWS, :] + own_part
    for k, ref in enumerate((o0, o1, o2, o3)):
        first = 64 * (core ^ (k % 2)) + 32 * (((sec >> 1) & 1) ^ (k // 2))
        ref[...] = res_ref[pl.ds(pl.multiple_of(first, 32), 32), :].astype(BF)


def slab_place(s):
    if s >= 8:
        return 15 - s, 0
    return s, 128 * (9 - (s // 2 + 1))


def recur_kernel(ints, sum_ref, mine_ref, other_ref, out_ref, slab_ref, pq_ref, h_ref, acc_ref, t_ref, pre_ref, ds_ref, ho_ref):
    core = ints[0]
    mine_row = pl.multiple_of(16 * core, 16)
    other_row = pl.multiple_of(16 * (1 - core), 16)
    for q in range(DP):
        base = 128 * (q // 4) + 32 * (q % 4)
        slab_ref[pl.ds(base + mine_row, 16), :] = mine_ref[q]
        slab_ref[pl.ds(base + other_row, 16), :] = other_ref[q]
    pq_ref[...] = jnp.zeros_like(pq_ref)
    pq_ref[0:8, :] = sum_ref[:, 0:3072]
    more = sum_ref[:, 3072:3584]
    for i in range(2):
        for k in range(4):
            pq_ref[8 + i : 9 + i, 512 * k : 512 * k + 512] = more[4 * i + k : 4 * i + k + 1]
    h_ref[...] = jnp.zeros_like(h_ref)
    acc_ref[...] = jnp.zeros_like(acc_ref)
    misc = sum_ref[:, 3584:3712]
    pair_lane = lax.broadcasted_iota(jnp.int32, (8, 128), 1) % 4 >= 2
    n_own = jnp.sum(jnp.where(pair_lane, 0.0, misc), axis=1, keepdims=True)
    n_pair = jnp.sum(jnp.where(pair_lane, misc, 0.0), axis=1, keepdims=True)
    n = jnp.concatenate([n_own, n_pair], axis=0)
    row = lax.broadcasted_iota(jnp.int32, (16, 1), 0)
    n = jnp.where(row < 10, n, 0.0)

    inverse = []
    zeros = jnp.zeros((16, RANK), BF)
    for s in range(SECT):
        place, off = slab_place(s)
        r0 = 128 * place
        depth = 128 * ((s + 1) // 2)
        tp = pq_ref[:, 128 * s : 128 * s + 64]
        tq = pq_ref[:, 128 * s + 64 : 128 * s + 128]
        if s:
            before = h_ref[:, 0:depth]
            tp = tp + dot(before, slab_ref[r0 : r0 + 64, off : off + depth], NT)
            tq = tq + dot(before, slab_ref[r0 + 64 : r0 + 128, off : off + depth], NT)
        inv = lax.rsqrt(jnp.maximum(n, 0.0) * (1.0 / D) + EPS)
        inverse.append(inv)
        pre = inv * tp
        sig = 0.5 + 0.5 * jnp.tanh(0.5 * pre)
        hf = pre * sig
        h = hf.astype(BF)
        pre_ref[:, 64 * s : 64 * s + 64] = pre
        ds_ref[:, 64 * s : 64 * s + 64] = sig * (1.0 + pre * (1.0 - sig))
        tile = slice(128 * (s // 2), 128 * (s // 2) + 128)
        own = jnp.concatenate([zeros, h] if s % 2 else [h, zeros], axis=1)
        h_ref[:, tile] = h_ref[:, tile] + own if s % 2 else own
        hd = dot(own, slab_ref[r0 + 64 : r0 + 128, off + tile.start : off + tile.stop], NT)
        n = n + jnp.sum(h.astype(F32) * (2.0 * tq + hd), axis=1, keepdims=True)
        t_ref[:, 64 * s : 64 * s + 64] = tq + hd

    lane16 = lax.broadcasted_iota(jnp.int32, (16, 128), 1)
    beta_sum = jnp.zeros((16, 1), F32)
    misc_out = jnp.zeros((16, 128), F32)
    for s in range(SECT - 1, -1, -1):
        place, off = slab_place(s)
        r0 = 128 * place
        cols = slice(64 * s, 64 * s + 64)
        inv = inverse[s]
        hf = h_ref[:, cols].astype(F32)
        dh = pq_ref[:, 2048 + 64 * s : 2048 + 64 * s + 64] + acc_ref[:, cols] - beta_sum * t_ref[:, cols]
        dp = (dh * ds_ref[:, cols]).astype(BF).astype(F32)
        beta = inv * inv * (jnp.sum(dp * pre_ref[:, cols], axis=1, keepdims=True) * (1.0 / D))
        z = (inv * dp).astype(BF)
        hb = (beta_sum * hf).astype(BF)
        depth = 128 * ((s + 1) // 2)
        for start in range(depth - 128, -1, -128):
            part = slice(start, start + 128)
            acc_ref[:, part] = (
                acc_ref[:, part]
                + dot(z, slab_ref[r0 : r0 + 64, off + start : off + start + 128], NN)
                - dot(hb, slab_ref[r0 + 64 : r0 + 128, off + start : off + start + 128], NN)
            )
        beta_sum = beta_sum + beta
        ho_ref[0:8, 1024 + 64 * s : 1024 + 64 * s + 64] = z[0:8].astype(F32)
        inv_hi, inv_lo = hi_lo(inv)
        misc_out = jnp.where(lane16 == s, beta, misc_out)
        misc_out = jnp.where(lane16 == 16 + s, inv_hi, misc_out)
        misc_out = jnp.where(lane16 == 32 + s, inv_lo, misc_out)
    h_all = h_ref[...].astype(F32)
    ho_ref[0:8, 0:1024] = h_all[0:8]
    for i in range(2):
        for k in range(4):
            ho_ref[4 * i + k : 4 * i + k + 1, 2048:2304] = h_all[8 + i : 9 + i, 256 * k : 256 * k + 256]
    extra_misc = pltpu.roll(misc_out[8:16], 32, 1)
    lane8 = lax.broadcasted_iota(jnp.int32, (8, 128), 1)
    row8 = lax.broadcasted_iota(jnp.int32, (8, 128), 0)
    keep = (lane8 >= 48) & (lane8 < 80) & (row8 < 2)
    ho_ref[0:8, 2304:2432] = jnp.where(keep, extra_misc, jnp.where(lane8 < 48, misc_out[0:8], 0.0))
    out_ref[...] = ho_ref[...].astype(BF)


def rebuild_kernel(ints, x_ref, pair_ref, mine_ref, other_ref, eh_ref, wc_ref, out_ref, back_ref):
    gather_rows(ints[3], mine_ref, other_ref, back_ref)
    own_at = pl.multiple_of(ints[0], 32)
    pair_at = pl.multiple_of(ints[1], 32)
    alive = ints[2] > 0
    x = x_ref[...].astype(F32)
    e = pair_ref[...].astype(F32)
    for s in range(SECT):
        out_ref[s, pl.ds(own_at, ROWS), :] = jnp.where(alive, x, 0.0).astype(BF)
        out_ref[s, pl.ds(pair_at, PAIR), :] = e.astype(BF)
        if s < SECT - 1:
            up = wc_ref[128 * s + 64 : 128 * s + 128, :]
            x = x + dot(back_ref[:, 64 * s : 64 * s + 64], up, NN)
            e = e + dot(eh_ref[:, 64 * s : 64 * s + 64], up, NN)


def gather_rows(core, mine_ref, other_ref, full_ref):
    full_ref[pl.ds(pl.multiple_of(64 * core, 64), 64), :] = mine_ref[...]
    full_ref[pl.ds(pl.multiple_of(64 * (1 - core), 64), 64), :] = other_ref[...]


def pick(values, index):
    out = values[0]
    for k in range(1, len(values)):
        out = jnp.where(index == k, values[k], out)
    return out


def grads_kernel(ints, x_ref, g_ref, mine_ref, other_ref, wc_ref, keep_ref, send_ref, back_ref, xs_ref, ht_ref, zt_ref):
    gather_rows(ints[0], mine_ref, other_ref, back_ref)
    along = ints[1]
    ht_ref[...] = back_ref[:, 0:1024].T
    zt_ref[...] = back_ref[:, 1024:2048].T
    x = x_ref[...].astype(F32)
    for s in range(SECT):
        xs_ref[s] = x.astype(BF)
        if s < SECT - 1:
            x = x + dot(back_ref[:, 64 * s : 64 * s + 64], wc_ref[128 * s + 64 : 128 * s + 128, :], NN)
    g = g_ref[...].astype(F32)
    betas = back_ref[:, 2304:2432].astype(F32)
    blocks = [None] * 4
    for s in range(SECT - 1, -1, -1):
        xs = xs_ref[s]
        up = dot(ht_ref[64 * s : 64 * s + 64, :], g.astype(BF), NN)
        down = dot(zt_ref[64 * s : 64 * s + 64, :], xs, NN)
        both = jnp.concatenate([up, down], axis=0).astype(BF)
        for h in range(2):
            blocks[2 * (s % 2) + h] = both[:, 128 * h : 128 * h + 128]
        if s % 2 == 0:
            for ref, flips in ((keep_ref, (0, 3)), (send_ref, (1, 2))):
                for k in range(2):
                    ref[k, place_z(s)] = pick(blocks, along ^ flips[k])
        if s:
            z = back_ref[:, 1024 + 64 * s : 1024 + 64 * s + 64]
            g = g + dot(z, wc_ref[128 * s : 128 * s + 64, :], NN) - betas[:, s : s + 1] * xs.astype(F32)


def join_kernel(in_ref, out_ref):
    for k in range(SECT):
        out_ref[0, 0, :, F * k : F * k + F] = in_ref[k]


def call(kernel, n_in, outs, scratch, flops, nbytes, with_ints=True):
    return pl.pallas_call(
        kernel,
        out_shape=outs,
        in_specs=([SMEM] if with_ints else []) + vmem(n_in),
        out_specs=jax.tree.map(lambda _: pl.BlockSpec(memory_space=pltpu.VMEM), outs),
        scratch_shapes=scratch,
        compiler_params=pltpu.CompilerParams(vmem_limit_bytes=VMEM_LIMIT),
        cost_estimate=pl.CostEstimate(flops=flops, bytes_accessed=nbytes, transcendentals=0),
    )


def shape(*dims, kind=BF):
    return jax.ShapeDtypeStruct(dims, kind)


def exchange(value, axis, groups=None):
    return lax.all_to_all(value, axis, 0, 0, tiled=True, axis_index_groups=groups)


def flip(value, bits):
    return lax.ppermute(value, "dp", [(i, i ^ bits) for i in range(DP)])


def scatter_sum(keep, send, me, later, finish):
    first = flip(send, 1)
    low = (me >> 2) & 1
    arrived = 0.0
    for e, b in ((1, 0), (0, 1), (1, 1)):
        part = keep[e].astype(F32) + first[e].astype(F32)
        part = lax.dynamic_index_in_dim(part.astype(BF).reshape(4, 2, 128, 128), low ^ b, 1, keepdims=False)
        arrived = arrived + flip(part, 3 * e | 4 * b).astype(F32)
    own = (keep[0].astype(F32) + first[0].astype(F32)).reshape(4, 2, 128, 128)
    value = lax.dynamic_index_in_dim(own, low, 1, keepdims=False) + arrived
    value, later = lax.optimization_barrier((value, later))
    later = finish(later)
    middle = (me >> 3) & 1
    value = value.reshape(2, 2, 128, 128)
    send = lax.dynamic_index_in_dim(value, 1 - middle, 1, keepdims=False).astype(BF)
    value = (lax.dynamic_index_in_dim(value, middle, 1, keepdims=False) + flip(send, 8).astype(F32)).astype(BF)
    value, later = lax.optimization_barrier((value, later))
    keep = lax.dynamic_index_in_dim(value, me >> 4, 0, keepdims=False)
    send = lax.dynamic_index_in_dim(value, 1 - (me >> 4), 0, keepdims=False)
    both = ("section", "dp")
    mine = lax.ppermute(keep, both, [(a, owner(a // DP, a % DP)) for a in range(SECT * DP)])
    theirs = lax.ppermute(send, both, [(a, owner(a // DP, a % DP ^ 16)) for a in range(SECT * DP)])
    return mine, theirs, later


def place_z(s):
    return (s // 2 - 2) % 8


def owner(sec, q):
    return (2 * ((q // 4 + 2) % 8) + q // 2 % 2) * DP + 2 * sec + q % 2


def body(x, g, worker, gain, narrow, widen):
    sec = lax.axis_index("section")
    me = lax.axis_index("dp")

    gain_here = lax.dynamic_slice(gain, (0, 128 * me), (1, 128))
    block = jnp.concatenate([(narrow[0].astype(F32) * gain_here).astype(BF), widen[0]], axis=0)
    block = lax.ppermute(block, ("section", "dp"), [(owner(a // DP, a % DP), a) for a in range(SECT * DP)])

    owners = jnp.arange(DP, dtype=jnp.int32)
    takers = worker[:, ::2]
    mine = lax.dynamic_index_in_dim(takers, me, 0, keepdims=False)
    alive = mine[0] == me
    comes = jnp.any((takers == me) & (owners != me)[:, None], axis=1)
    source = jnp.sum(jnp.where(comes, owners, 0))
    taking = jnp.any(comes)
    pair_first = taking & (source < me)
    goes = (mine[None, :] == owners[:, None]) & jnp.logical_not(alive)
    quads = jnp.concatenate([x[:, 0:128].reshape(4, PAIR, 128), x[:, 128:256].reshape(4, PAIR, 128)], axis=1)
    outgoing = jnp.zeros((DP, 2 * PAIR, 128), BF)
    for j in range(4):
        outgoing = jnp.where(goes[:, j][:, None, None], quads[j][None], outgoing)
    weights = jnp.concatenate([jnp.broadcast_to(block[None], (DP, 128, 128)), outgoing], axis=1)
    weights = exchange(weights, "dp")

    core = sec % 2
    ints = jnp.stack([me // 4, me % 4, core, source, taking.astype(jnp.int32), sec]).astype(jnp.int32)
    gkeep, gsend, wc, uc, pair = call(
        gram_kernel,
        1,
        (shape(16, GW), shape(16, GW), shape(2048, F), shape(1024, F), shape(PAIR, F)),
        [pltpu.VMEM((32, GW), F32)],
        10**8,
        3 * 10**6,
    )(ints, weights)
    swap = [(i, i ^ 1) for i in range(SECT)]
    share = (gkeep.astype(F32) + lax.ppermute(gsend, "section", swap).astype(F32)).astype(BF)
    parts = call(
        project_kernel,
        5,
        (shape(32, PIECE),) * 4,
        [pltpu.VMEM((ROWS, PIECE), F32), pltpu.VMEM((4 * ROWS, 128), F32)],
        3 * 10**8,
        3 * 10**6,
    )(ints, x, pair, g, wc, uc)
    share = exchange(jnp.broadcast_to(share[None], (8, 16, GW)), "section", Y_GROUPS)
    share = jnp.sum(share.astype(F32), axis=0).astype(BF)
    half = exchange(jnp.broadcast_to(share[None], (DP, 16, GW)), "dp")

    rows = parts[0].astype(F32)
    for k in range(1, 4):
        rows = rows + lax.ppermute(parts[k], "section", [(i, i ^ k) for i in range(SECT)]).astype(F32)
    rows = rows.astype(BF).reshape(4, 8, PIECE)
    here = sec // 4
    total = lax.dynamic_index_in_dim(rows, here, 0, keepdims=False).astype(F32)
    for k in range(1, 4):
        send = lax.dynamic_index_in_dim(rows, here ^ k, 0, keepdims=False)
        total = total + lax.ppermute(send, "section", [(i, i ^ (4 * k)) for i in range(SECT)]).astype(F32)
    half, total = lax.optimization_barrier((half, total))
    other = lax.ppermute(half, "section", swap)

    back = call(
        recur_kernel,
        3,
        shape(8, BACK),
        [
            pltpu.VMEM((1024, GW), BF),
            pltpu.VMEM((16, 3072), F32),
            pltpu.VMEM((16, 1024), BF),
            pltpu.VMEM((16, 1024), F32),
            pltpu.VMEM((16, 1024), F32),
            pltpu.VMEM((16, 1024), F32),
            pltpu.VMEM((16, 1024), F32),
            pltpu.VMEM((8, BACK), F32),
        ],
        2 * 10**8,
        3 * 10**6,
    )(core.reshape(1).astype(jnp.int32), total, half, other)
    back = exchange(jnp.broadcast_to(back[None], (8, 8, BACK)), "section", Y_GROUPS).reshape(64, BACK)
    back_other = lax.ppermute(back, "section", swap)

    blocks = call(
        grads_kernel,
        5,
        (shape(2, 8, 128, 128),) * 2,
        [
            pltpu.VMEM((ROWS, BACK), BF),
            pltpu.VMEM((SECT, ROWS, F), BF),
            pltpu.VMEM((1024, ROWS), BF),
            pltpu.VMEM((1024, ROWS), BF),
        ],
        3 * 10**8,
        3 * 10**6,
    )(jnp.stack([core, me % 4]).astype(jnp.int32), x, g, back, back_other, wc)

    small, small_other = back[:, 2048:2432], back_other[:, 2048:2432]
    small = jnp.where(
        core == 0, jnp.concatenate([small, small_other], axis=0), jnp.concatenate([small_other, small], axis=0)
    ).reshape(SECT, 8, 384)
    extra_h = small[:, :, 0:256].reshape(SECT, 2, 4, 256).transpose(1, 0, 2, 3).reshape(PAIR, 1024)
    own_at = jnp.where(pair_first, PAIR, 0)
    pair_at = jnp.where(pair_first, 0, ROWS)
    rows_out = call(
        rebuild_kernel,
        6,
        shape(SECT, ROWS + PAIR, F),
        [pltpu.VMEM((ROWS, BACK), BF)],
        2 * 10**8,
        3 * 10**6,
    )(jnp.stack([own_at, pair_at, alive.astype(jnp.int32), core]).astype(jnp.int32), x, pair, back, back_other, extra_h, wc)
    saved = exchange(rows_out, "section")
    def slot_rstd(misc):
        misc = misc.astype(F32)
        own_inv = misc[:, :, 16:32] + misc[:, :, 32:48]
        pair_inv = misc[:, 0:2, 48:64] + misc[:, 0:2, 64:80]
        own_inv = lax.dynamic_index_in_dim(own_inv, sec, 2, keepdims=False).reshape(ROWS)
        pair_inv = lax.dynamic_index_in_dim(pair_inv, sec, 2, keepdims=False).T.reshape(PAIR)
        own_inv = jnp.where(alive, own_inv, 0.0)
        pair_inv = jnp.where(taking, pair_inv, 0.0)
        return jnp.where(
            pair_first, jnp.concatenate([pair_inv, own_inv]), jnp.concatenate([own_inv, pair_inv])
        ).reshape(1, 1, ROWS + PAIR)

    mine_sum, other_sum, rstd = scatter_sum(*blocks, me, small[:, :, 256:384], slot_rstd)
    saved = call(join_kernel, 1, shape(1, 1, ROWS + PAIR, D), [], 0, 3 * 10**6, False)(saved)

    saved, mine_sum, other_sum = lax.optimization_barrier((saved, mine_sum, other_sum))
    grads = mine_sum.astype(F32) + other_sum.astype(F32)

    return rstd, saved, (grads[64:128] * gain_here)[None], grads[0:64][None]


def solution(mesh):
    in_specs = (
        P("dp", "section"),
        P("dp", "section"),
        P(),
        P("section", None),
        P("section", None, "dp"),
        P("section", None, "dp"),
    )
    out_specs = (
        P("section", "dp", None),
        P("section", "dp", None, None),
        P("section", None, "dp"),
        P("section", None, "dp"),
    )
    return jax.shard_map(body, mesh=mesh, in_specs=in_specs, out_specs=out_specs, check_vma=False)
```
